32 devices in a mesh: groups: 2 (over y), pulse: 4 (over x, core), range: 4 (over z).
Axes of the slice: x: 2, y: 2, z: 4, core: 2. Of those that a mesh axis runs over, the one named last changes fastest.
Arguments:
- echoes: bfloat16 [2048, 2, 8192], P(('groups', 'pulse'), None, 'range'), parts along dimension 0, may hold values from -6 to 6
- shifts: int32 [2048], P(('groups', 'pulse')), parts along dimension 0, may hold values from -64 to 64
- tap_weights: float32 [2048, 8], P(('groups', 'pulse')), parts along dimension 0, may hold values from -2 to 2
- angles: float32 [2048], P(('groups', 'pulse')), parts along dimension 0, may hold values from -3.140625 to 3.140625
- slopes: float32 [2048], P(('groups', 'pulse')), parts along dimension 0, may hold values from -0.05 to 0.05
- steering: bfloat16 [2, 8, 32], replicated, may hold values from -0.75 to 0.75
- footprint: int32 [32, 32], P('groups'), parts along dimension 0, may hold values from 0 to 255, as said below
- tile_coeffs: bfloat16 [32, 2, 64, 32], P(('groups', 'pulse')), parts along dimension 0, may hold values from -0.75 to 0.75
Outputs:
- image_tiles: bfloat16 [32, 2, 64, 8192], P(('groups', 'pulse'), None, None, 'range'), parts along dimension 0
The draws below stay inside these ranges and needn't reach their ends.
There are 2 independent parts, one for each index of `groups`. The reference program is written for one: setup_inputs(seed, part) draws one part's arguments, and reference() takes and returns one part's arrays. A program takes and returns all parts, laid end to end along the dimension named above; an argument that names none is the same for every part. Nothing has to cross between parts.
Inputs may be any that keep to these rules, and one draw needn't show every extreme that they name: `footprint`: beam s * 8 + b belongs to subaperture s. The 128 entries of tiles k * 4 to k * 4 + 3 are distinct beams; at most 64 of them lie in any one range of beams j * 64 to j * 64 + 63, and for every k exactly 64 lie in some such range.
All inputs are finite; a program needn't handle non-finite values.
Results may differ from the reference program's by a relative error of at most 0.0058.
Values may be sent and summed in bfloat16 or wider, within the bound.
A program may use at most 64 MiB of HBM per device.

```python
import jax
import jax.numpy as jnp
from jax import lax

SUB = 32
BEAMS = 8
TAPS = 8
MAXS = 64
TILE_DEV = 4
FOOT = 32
AZ = 64
PULSES = 1024
RANGE = 8192
NT = 16
BEAM_DEV = 64
NBEAMS = 256
ENT = 128
CAP = 64
HALO = 68
N_PULSE = 4


def draw_footprint(key, part):
    average = ENT // N_PULSE

    def one_owner(owner):
        owner_key = jax.random.fold_in(key, owner)
        k_pairs, k_order, k_pick, k_mix = jax.random.split(owner_key, 4)
        spread = jax.random.randint(k_pairs, (N_PULSE // 2,), 0, average // 2 + 1)
        spread = spread.at[0].set(average)
        counts = jnp.stack([average + spread, average - spread], axis=1).reshape(N_PULSE)
        counts = counts[jax.random.permutation(k_order, N_PULSE)]

        def one_source(source):
            beam_order = jax.random.permutation(jax.random.fold_in(k_pick, source), BEAM_DEV)
            return source * BEAM_DEV + beam_order[:CAP]
        candidates = jax.vmap(one_source)(jnp.arange(N_PULSE, dtype=jnp.int32))
        is_valid = jnp.arange(CAP)[None, :] < counts[:, None]
        flat_ids = candidates.reshape(N_PULSE * CAP)
        flat_valid = is_valid.reshape(N_PULSE * CAP)
        ranking = jnp.argsort(jnp.where(flat_valid, 0, 1), stable=True)[:ENT]
        chosen = flat_ids[ranking]
        return chosen[jax.random.permutation(k_mix, ENT)].reshape(TILE_DEV, FOOT)
    owners = jax.vmap(one_owner)(jnp.arange(N_PULSE, dtype=jnp.int32))
    return owners.reshape(N_PULSE * TILE_DEV, FOOT).astype(jnp.int32)


def touch_ends(drawn, own_key, low, high):
    longest = drawn.shape.index(max(drawn.shape))
    spots = []
    for shift in (0, 1):
        where = [jax.random.randint(jax.random.fold_in(own_key, axis), (), 0, length) for axis, length in enumerate(drawn.shape)]
        where[longest] = (where[longest] + shift) % drawn.shape[longest]
        spots.append(tuple(where))
    return drawn.at[spots[0]].set(low).at[spots[1]].set(high)


def levels(stream_key, dims, cuts, smallest, largest):
    gain = 1.0
    for position, blocks in cuts:
        draws = jax.random.uniform(jax.random.fold_in(jax.random.fold_in(stream_key, 6), position), (blocks,), jnp.float32, smallest / len(cuts), largest / len(cuts))
        gain = gain * jnp.repeat(jnp.exp(draws), dims[position] // blocks).reshape((-1,) + (1,) * (len(dims) - 1 - position))
    return gain


def normal_values(key, shape, width, bound, cuts=(), kind=jnp.bfloat16):
    array = jax.random.normal(key, shape, jnp.float32) * width
    if len(cuts) > 0:
        array = levels(key, shape, cuts, -0.22, 0.18) * array
    return jnp.clip(array, min=-bound, max=bound).astype(kind)


def setup_inputs(seed: int = 0, part: int = 0) -> dict:
    arg_keys = jax.random.split(jax.random.key(seed), 9)
    own_keys = jax.random.split(jax.random.fold_in(arg_keys[8], part), 9)
    echoes = normal_values(own_keys[0], (PULSES, 2, RANGE), 1.0, 6.0, ((0, 4), (2, 4)))
    shifts = touch_ends(jax.random.randint(own_keys[1], (PULSES,), 0 - MAXS, MAXS + 1), jax.random.fold_in(own_keys[1], 1), 0 - MAXS, MAXS).astype(jnp.int32)
    tap_weights = normal_values(own_keys[2], (PULSES, TAPS), 0.35, 2.0, ((0, 4),), jnp.float32)
    angles = jnp.clip(jax.random.uniform(own_keys[3], (PULSES,), jnp.float32, -3.140625, 3.140625), -3.140625, 3.140625)
    slopes = jnp.clip(jax.random.uniform(own_keys[4], (PULSES,), jnp.float32, -0.05, 0.05) * levels(own_keys[4], (PULSES,), ((0, 4),), -0.4, 0.0), -0.05, 0.05)
    steering = normal_values(arg_keys[5], (2, BEAMS, SUB), (2 * SUB) ** -0.5, 0.75)
    footprint = draw_footprint(jax.random.fold_in(jax.random.fold_in(arg_keys[8], part), 71), part)
    tile_coeffs = normal_values(own_keys[7], (NT, 2, AZ, FOOT), (2 * FOOT) ** -0.5, 0.75, ((0, 4),))
    return {"echoes": echoes, "shifts": shifts, "tap_weights": tap_weights, "angles": angles, "slopes": slopes, "steering": steering, "footprint": footprint, "tile_coeffs": tile_coeffs}


def align_pulse(pulse_row, bin_offset, tap_row, phase_zero, phase_slope, start_cell):
    span_cells = pulse_row.shape[1] - 2 * HALO
    first_cell = (HALO + bin_offset - TAPS // 2 + 1).astype(jnp.int32)
    window = lax.dynamic_slice(pulse_row, (jnp.int32(0), first_cell), (2, span_cells + TAPS - 1)).astype(jnp.float32)
    summed = jnp.zeros((2, span_cells), jnp.float32)
    for tap_index in range(TAPS):
        summed = summed + tap_row[tap_index] * window[:, tap_index:tap_index + span_cells]
    positions = (start_cell + jnp.arange(span_cells)).astype(jnp.float32)
    phases = phase_zero + phase_slope * positions
    cosine_values = jnp.cos(phases)
    sine_values = jnp.sin(phases)
    real_part = cosine_values * summed[0] - sine_values * summed[1]
    imag_part = sine_values * summed[0] + cosine_values * summed[1]
    return jnp.stack([real_part, imag_part]).astype(jnp.bfloat16)


def reference(echoes, shifts, tap_weights, angles, slopes, steering, footprint, tile_coeffs):
    padded = jnp.pad(echoes, ((0, 0), (0, 0), (HALO, HALO)))
    aligner = jax.vmap(align_pulse, in_axes=(0, 0, 0, 0, 0, None))

    def one_sub(sub_index):
        first_pulse = (sub_index * SUB).astype(jnp.int32)
        rows = lax.dynamic_slice_in_dim(padded, first_pulse, SUB, 0)
        offsets = lax.dynamic_slice_in_dim(shifts, first_pulse, SUB, 0)
        tap_rows = lax.dynamic_slice_in_dim(tap_weights, first_pulse, SUB, 0)
        zeros_at = lax.dynamic_slice_in_dim(angles, first_pulse, SUB, 0)
        slope_at = lax.dynamic_slice_in_dim(slopes, first_pulse, SUB, 0)
        aligned = aligner(rows, offsets, tap_rows, zeros_at, slope_at, jnp.int32(0))
        real_in = aligned[:, 0]
        imag_in = aligned[:, 1]
        real_part = jnp.dot(steering[0], real_in, preferred_element_type=jnp.float32) - jnp.dot(steering[1], imag_in, preferred_element_type=jnp.float32)
        imag_part = jnp.dot(steering[0], imag_in, preferred_element_type=jnp.float32) + jnp.dot(steering[1], real_in, preferred_element_type=jnp.float32)
        return jnp.stack([real_part, imag_part], axis=1).astype(jnp.bfloat16)

    beam_rows = lax.map(one_sub, jnp.arange(PULSES // SUB, dtype=jnp.int32))
    beam_rows = beam_rows.reshape(NBEAMS, 2, RANGE)

    def one_tile(pair):
        beam_ids, tile_coeff = pair
        picked = jnp.take(beam_rows, beam_ids, axis=0).astype(jnp.float32)
        weights = tile_coeff.astype(jnp.float32)
        real_part = jnp.einsum('af,fw->aw', weights[0], picked[:, 0]) - jnp.einsum('af,fw->aw', weights[1], picked[:, 1])
        imag_part = jnp.einsum('af,fw->aw', weights[0], picked[:, 1]) + jnp.einsum('af,fw->aw', weights[1], picked[:, 0])
        return jnp.stack([real_part, imag_part]).astype(jnp.bfloat16)

    return lax.map(one_tile, (footprint, tile_coeffs))
```

```python
import functools

import jax
import jax.numpy as jnp
from jax import lax
from jax.experimental import pallas as pl
from jax.experimental.pallas import tpu as pltpu
from jax.sharding import PartitionSpec as P

SUB = 32
BEAMS = 8
TAPS = 8
TILE_DEV = 4
FOOT = 32
AZ = 64
LANES = 128
F32 = jnp.float32
BF16 = jnp.bfloat16
MESH_ID = pl.DeviceIdType.MESH
UNROLL = 8


def beam_kernel(
    n_pulse, n_range, blocks, subs,
    shifts, echoes, heads, tails, params, steering, footprint, tile_coeffs,
    gathered, dense,
    cells, left, right, left_f, right_f, rolled, y_re, y_im, taps_out, sent,
    lhs_re, lhs_im, e_re, e_im, d_re, d_im, reach,
    load_sem, halo_send, halo_recv, own_sem,
    x_send, x_recv, sib_send, sib_recv, fwd_send, fwd_recv,
):
    chips = n_pulse // 2
    me = lax.axis_index("pulse")
    zi = lax.axis_index("range")
    gi = lax.axis_index("groups")
    chip = me // 2
    core = me % 2
    sibling = chip * 2 + (1 - core)
    pulses = subs * SUB
    has_left = zi > 0
    has_right = zi < n_range - 1

    def dev(p, z):
        return (gi, p, z)

    load = pltpu.make_async_copy(echoes, cells, load_sem)
    load.start()

    barrier = pltpu.get_barrier_semaphore()
    pl.semaphore_signal(barrier, inc=1, device_id=dev(sibling, zi), device_id_type=MESH_ID)
    for d in range(1, chips):
        peer = ((chip + d) % chips) * 2 + core
        pl.semaphore_signal(barrier, inc=1, device_id=dev(peer, zi), device_id_type=MESH_ID)

    @pl.when(has_left)
    def _():
        pl.semaphore_signal(barrier, inc=1, device_id=dev(me, zi - 1), device_id_type=MESH_ID)

    @pl.when(has_right)
    def _():
        pl.semaphore_signal(barrier, inc=1, device_id=dev(me, zi + 1), device_id_type=MESH_ID)

    pl.semaphore_wait(barrier, chips + jnp.minimum(zi, 1) + jnp.minimum(n_range - 1 - zi, 1))

    def to_left():
        return pltpu.make_async_remote_copy(
            src_ref=heads, dst_ref=right, send_sem=halo_send.at[0], recv_sem=halo_recv.at[0],
            device_id=dev(me, zi - 1), device_id_type=MESH_ID)

    def to_right():
        return pltpu.make_async_remote_copy(
            src_ref=tails, dst_ref=left, send_sem=halo_send.at[1], recv_sem=halo_recv.at[1],
            device_id=dev(me, zi + 1), device_id_type=MESH_ID)

    @pl.when(has_left)
    def _():
        to_left().start()

    @pl.when(has_right)
    def _():
        to_right().start()

    lane = lax.broadcasted_iota(jnp.int32, (LANES, LANES), 1).astype(F32)
    start = (zi * (blocks * LANES)).astype(F32)
    for h in range(pulses // LANES):
        span = pl.ds(h * LANES, LANES)

        def column(row):
            return jnp.transpose(jnp.broadcast_to(params[row:row + 1, span], (LANES, LANES)))

        angle, slope, shift = column(TAPS), column(TAPS + 1), column(TAPS + 2)
        phase = angle + slope * (start + lane)
        e_re[span, :] = jnp.cos(phase)
        e_im[span, :] = jnp.sin(phase)
        step = slope * float(LANES)
        d_re[span, :] = jnp.cos(step)
        d_im[span, :] = jnp.sin(step)
        reach[span, :] = shift + lane + float(LANES - TAPS // 2 + 1)

    tap_phase = params[TAPS + 1:TAPS + 2, :] * lax.broadcasted_iota(jnp.int32, (TAPS, pulses), 0).astype(F32)
    tap_re = params[0:TAPS, :] * jnp.cos(tap_phase)
    tap_im = -params[0:TAPS, :] * jnp.sin(tap_phase)
    st_re = steering[0].astype(F32)
    st_im = steering[1].astype(F32)
    for s in range(subs):
        g_re = tap_re[:, s * SUB:(s + 1) * SUB]
        g_im = tap_im[:, s * SUB:(s + 1) * SUB]
        for k in range(TAPS):
            w_re = st_re * g_re[k:k + 1] - st_im * g_im[k:k + 1]
            w_im = st_re * g_im[k:k + 1] + st_im * g_re[k:k + 1]
            rows = pl.ds(k * 2 * BEAMS, 2 * BEAMS)
            lhs_re[s, rows, :] = jnp.concatenate([w_re, w_im], axis=0).astype(BF16)
            lhs_im[s, rows, :] = jnp.concatenate([-w_im, w_re], axis=0).astype(BF16)

    @pl.when(has_left)
    def _():
        to_right().wait_recv()

    @pl.when(has_right)
    def _():
        to_left().wait_recv()

    @pl.when(jnp.logical_not(has_left))
    def _():
        left[...] = jnp.zeros(left.shape, BF16)

    @pl.when(jnp.logical_not(has_right))
    def _():
        right[...] = jnp.zeros(right.shape, BF16)

    left_f[...] = left[...].astype(F32)
    right_f[...] = right[...].astype(F32)
    load.wait()

    def x_copy(d, s):
        peer = ((chip + d) % chips) * 2 + core
        return pltpu.make_async_remote_copy(
            src_ref=sent.at[s], dst_ref=gathered.at[me, s],
            send_sem=x_send.at[d - 1, s], recv_sem=x_recv.at[d - 1, s],
            device_id=dev(peer, zi), device_id_type=MESH_ID)

    def sib_copy(s):
        return pltpu.make_async_remote_copy(
            src_ref=sent.at[s], dst_ref=gathered.at[me, s],
            send_sem=sib_send.at[s], recv_sem=sib_recv.at[s],
            device_id=dev(sibling, zi), device_id_type=MESH_ID)

    def fwd_copy(d, s):
        owner = ((chip + chips - d) % chips) * 2 + core
        return pltpu.make_async_remote_copy(
            src_ref=gathered.at[owner, s], dst_ref=gathered.at[owner, s],
            send_sem=fwd_send.at[d - 1, s], recv_sem=fwd_recv.at[d - 1, s],
            device_id=dev(sibling, zi), device_id_type=MESH_ID)

    def own_copy(s):
        return pltpu.make_async_copy(sent.at[s], gathered.at[me, s], own_sem.at[s])

    def forward(s):
        for d in range(1, chips):
            x_copy(d, s).wait_recv()
            fwd_copy(d, s).start()

    own_rows = 2 * blocks

    def one_sub(s, carry):
        def some_pulses(group, inner):
            for u in range(UNROLL):
                j = group * UNROLL + u
                pulse = s * SUB + j
                amount = (LANES - (shifts[pulse] + (LANES - TAPS // 2 + 1))) & (LANES - 1)
                rolled[0:own_rows, j, :] = pltpu.roll(cells[pulse].astype(F32), amount, axis=1)
                rolled[own_rows:own_rows + 2, j, :] = pltpu.roll(left_f[pl.ds(2 * pulse, 2), :], amount, axis=1)
                rolled[own_rows + 2:own_rows + 4, j, :] = pltpu.roll(right_f[pl.ds(2 * pulse, 2), :], amount, axis=1)
            return inner

        lax.fori_loop(0, SUB // UNROLL, some_pulses, 0)

        rows = pl.ds(pl.multiple_of(s * SUB, SUB), SUB)
        at = reach[rows, :]
        first = at < float(LANES)
        second = at < float(2 * LANES)
        turn_re, turn_im = d_re[rows, :], d_im[rows, :]
        now_re, now_im = e_re[rows, :], e_im[rows, :]

        def block(b, c):
            b = min(b, blocks + 1)
            where = own_rows if b == 0 else own_rows + 2 if b == blocks + 1 else 2 * (b - 1)
            return rolled[where + c]

        for b in range(blocks + 1):
            z = [
                jnp.where(first, block(b, c), jnp.where(second, block(b + 1, c), block(b + 2, c)))
                for c in range(2)
            ]
            span = slice(b * LANES, (b + 1) * LANES)
            y_re[:, span] = (now_re * z[0] - now_im * z[1]).astype(BF16)
            y_im[:, span] = (now_im * z[0] + now_re * z[1]).astype(BF16)
            now_re, now_im = now_re * turn_re - now_im * turn_im, now_im * turn_re + now_re * turn_im

        taps_out[...] = jnp.dot(lhs_re[s], y_re[...], preferred_element_type=F32) + jnp.dot(
            lhs_im[s], y_im[...], preferred_element_type=F32)
        width = (blocks + 1) * LANES
        total = taps_out[0:2 * BEAMS, :]
        for k in range(1, TAPS):
            total = total + pltpu.roll(taps_out[k * 2 * BEAMS:(k + 1) * 2 * BEAMS, :], width - k, axis=1)
        sent[s] = total[:, :blocks * LANES].astype(BF16)

        for d in range(1, chips):
            x_copy(d, s).start()
        sib_copy(s).start()
        own_copy(s).start()

        @pl.when(s >= 2)
        def _():
            forward(s - 2)

        return carry

    lax.fori_loop(0, subs, one_sub, 0)
    forward(subs - 2)

    n_rows = n_pulse * subs * 2 * BEAMS
    row = lax.broadcasted_iota(jnp.int32, (n_rows, FOOT), 0)
    beam = (row // (2 * BEAMS)) * BEAMS + row % BEAMS
    is_im = (row // BEAMS) % 2
    for t in range(TILE_DEV):
        ids = footprint[pl.ds(me * TILE_DEV + t, 1), :]
        hit = beam == ids
        hot_re = jnp.where(hit & (is_im == 0), 1.0, 0.0).astype(BF16)
        hot_im = jnp.where(hit & (is_im == 1), 1.0, 0.0).astype(BF16)
        c_re, c_im = tile_coeffs[t, 0], tile_coeffs[t, 1]

        def spread(a, b):
            return lax.dot_general(a, b, (((1,), (1,)), ((), ())), preferred_element_type=F32)

        dense[t * 2 * AZ:t * 2 * AZ + AZ, :] = (spread(c_re, hot_re) - spread(c_im, hot_im)).astype(BF16)
        dense[t * 2 * AZ + AZ:(t + 1) * 2 * AZ, :] = (spread(c_im, hot_re) + spread(c_re, hot_im)).astype(BF16)

    forward(subs - 1)

    def finish(s, carry):
        own_copy(s).wait()
        sib_copy(s).wait()
        for d in range(1, chips):
            x_copy(d, s).wait_send()
            fwd_copy(d, s).wait()
        return carry

    lax.fori_loop(0, subs, finish, 0)

    @pl.when(has_left)
    def _():
        to_left().wait_send()

    @pl.when(has_right)
    def _():
        to_right().wait_send()


def project_kernel(dense, beams, out):
    out[...] = jnp.dot(dense[...], beams[...], preferred_element_type=F32).astype(BF16)


def body(n_pulse, n_range, echoes, shifts, tap_weights, angles, slopes, steering, footprint, tile_coeffs):
    pulses, _, width = echoes.shape
    blocks = width // LANES
    subs = pulses // SUB
    chips = n_pulse // 2
    by_block = echoes.reshape(pulses, 2, blocks, LANES).transpose(0, 2, 1, 3).reshape(pulses, 2 * blocks, LANES)
    heads = echoes[:, :, :LANES].reshape(2 * pulses, LANES)
    tails = echoes[:, :, width - LANES:].reshape(2 * pulses, LANES)
    params = jnp.concatenate(
        [
            tap_weights.T, angles[None], slopes[None], shifts[None].astype(F32),
            jnp.zeros((5, pulses), F32),
        ],
        axis=0,
    )
    n_rows = n_pulse * subs * 2 * BEAMS
    out_rows = TILE_DEV * 2 * AZ
    vmem = pl.BlockSpec(memory_space=pltpu.VMEM)
    hbm = pl.BlockSpec(memory_space=pl.ANY)
    dma = pltpu.SemaphoreType.DMA
    gathered, dense = pl.pallas_call(
        functools.partial(beam_kernel, n_pulse, n_range, blocks, subs),
        out_shape=(
            jax.ShapeDtypeStruct((n_pulse, subs, 2 * BEAMS, width), BF16),
            jax.ShapeDtypeStruct((out_rows, n_rows), BF16),
        ),
        in_specs=[pl.BlockSpec(memory_space=pltpu.SMEM), hbm, vmem, vmem, vmem, vmem, vmem, vmem],
        out_specs=(hbm, vmem),
        scratch_shapes=[
            pltpu.VMEM((pulses, 2 * blocks, LANES), BF16),
            pltpu.VMEM((2 * pulses, LANES), BF16),
            pltpu.VMEM((2 * pulses, LANES), BF16),
            pltpu.VMEM((2 * pulses, LANES), F32),
            pltpu.VMEM((2 * pulses, LANES), F32),
            pltpu.VMEM((2 * blocks + 4, SUB, LANES), F32),
            pltpu.VMEM((SUB, width + LANES), BF16),
            pltpu.VMEM((SUB, width + LANES), BF16),
            pltpu.VMEM((TAPS * 2 * BEAMS, width + LANES), F32),
            pltpu.VMEM((subs, 2 * BEAMS, width), BF16),
            pltpu.VMEM((subs, TAPS * 2 * BEAMS, SUB), BF16),
            pltpu.VMEM((subs, TAPS * 2 * BEAMS, SUB), BF16),
            pltpu.VMEM((pulses, LANES), F32),
            pltpu.VMEM((pulses, LANES), F32),
            pltpu.VMEM((pulses, LANES), F32),
            pltpu.VMEM((pulses, LANES), F32),
            pltpu.VMEM((pulses, LANES), F32),
            dma(()),
            dma((2,)),
            dma((2,)),
            dma((subs,)),
            dma((chips - 1, subs)),
            dma((chips - 1, subs)),
            dma((subs,)),
            dma((subs,)),
            dma((chips - 1, subs)),
            dma((chips - 1, subs)),
        ],
        compiler_params=pltpu.CompilerParams(
            collective_id=0, has_side_effects=True, vmem_limit_bytes=48 * 1024 * 1024
        ),
    )(shifts, by_block, heads, tails, params, steering, footprint, tile_coeffs)

    columns = 512
    image = pl.pallas_call(
        project_kernel,
        grid=(width // columns,),
        out_shape=jax.ShapeDtypeStruct((out_rows, width), BF16),
        in_specs=[
            pl.BlockSpec((out_rows, n_rows), lambda i: (0, 0)),
            pl.BlockSpec((n_rows, columns), lambda i: (0, i)),
        ],
        out_specs=pl.BlockSpec((out_rows, columns), lambda i: (0, i)),
        compiler_params=pltpu.CompilerParams(vmem_limit_bytes=48 * 1024 * 1024),
    )(dense, gathered.reshape(n_rows, width))
    return image.reshape(TILE_DEV, 2, AZ, width)


def solution(mesh):
    placed = (
        P(("groups", "pulse"), None, "range"),
        P(("groups", "pulse")),
        P(("groups", "pulse"), None),
        P(("groups", "pulse")),
        P(("groups", "pulse")),
        P(),
        P("groups", None),
        P(("groups", "pulse"), None, None, None),
    )
    return jax.shard_map(
        functools.partial(body, mesh.shape["pulse"], mesh.shape["range"]),
        mesh=mesh,
        in_specs=placed,
        out_specs=P(("groups", "pulse"), None, None, "range"),
        check_vma=False,
    )
```

```python
import functools

import jax
import jax.numpy as jnp
from jax import lax
from jax.experimental import pallas as pl
from jax.experimental.pallas import tpu as pltpu
from jax.sharding import PartitionSpec as P

SUB = 32
BEAMS = 8
TAPS = 8
TILE_DEV = 4
FOOT = 32
AZ = 64
LANES = 128
F32 = jnp.float32
BF16 = jnp.bfloat16
MESH_ID = pl.DeviceIdType.MESH
UNROLL = 8


def beam_kernel(
    n_pulse, n_range, blocks, subs,
    echoes_in, shifts_in, taps_in, angles_in, slopes_in, steering_in, footprint_in, coeffs_in, heads, tails,
    gathered, dense,
    cells, shifts, shift_row, taps, angles, slopes, steering, footprint, coeffs,
    left, right, left_f, right_f, rolled, y, taps_out, sent,
    lhs, e_re, e_im, d_re, d_im, reach,
    load_sem, halo_send, halo_recv, own_sem,
    x_send, x_recv, sib_send, sib_recv, fwd_send, fwd_recv,
):
    chips = n_pulse // 2
    me = lax.axis_index("pulse")
    zi = lax.axis_index("range")
    gi = lax.axis_index("groups")
    chip = me // 2
    core = me % 2
    sibling = chip * 2 + (1 - core)
    pulses = subs * SUB
    has_left = zi > 0
    has_right = zi < n_range - 1

    def dev(p, z):
        return (gi, p, z)

    loads = [
        pltpu.make_async_copy(source, target, load_sem.at[n])
        for n, (source, target) in enumerate([
            (slopes_in, slopes), (taps_in, taps), (steering_in, steering), (angles_in, angles),
            (shifts_in, shift_row), (shifts_in, shifts), (echoes_in, cells),
            (footprint_in, footprint), (coeffs_in, coeffs),
        ])
    ]
    for load in loads:
        load.start()

    barrier = pltpu.get_barrier_semaphore()
    pl.semaphore_signal(barrier, inc=1, device_id=dev(sibling, zi), device_id_type=MESH_ID)
    for d in range(1, chips):
        peer = ((chip + d) % chips) * 2 + core
        pl.semaphore_signal(barrier, inc=1, device_id=dev(peer, zi), device_id_type=MESH_ID)

    @pl.when(has_left)
    def _():
        pl.semaphore_signal(barrier, inc=1, device_id=dev(me, zi - 1), device_id_type=MESH_ID)

    @pl.when(has_right)
    def _():
        pl.semaphore_signal(barrier, inc=1, device_id=dev(me, zi + 1), device_id_type=MESH_ID)

    for load in loads[:3]:
        load.wait()
    tap_phase = slopes[...] * lax.broadcasted_iota(jnp.int32, (TAPS, pulses), 0).astype(F32)
    tap_re = taps[...] * jnp.cos(tap_phase)
    tap_im = -taps[...] * jnp.sin(tap_phase)
    weights = steering[...].astype(F32)
    st_re, st_im = weights[0:BEAMS], weights[BEAMS:2 * BEAMS]
    for s in range(subs):
        g_re = tap_re[:, s * SUB:(s + 1) * SUB]
        g_im = tap_im[:, s * SUB:(s + 1) * SUB]
        for k in range(TAPS):
            w_re = st_re * g_re[k:k + 1] - st_im * g_im[k:k + 1]
            w_im = st_re * g_im[k:k + 1] + st_im * g_re[k:k + 1]
            both = jnp.concatenate(
                [jnp.concatenate([w_re, -w_im], axis=1), jnp.concatenate([w_im, w_re], axis=1)], axis=0)
            lhs[s, k * 2 * BEAMS:(k + 1) * 2 * BEAMS, :] = both.astype(BF16)

    pl.semaphore_wait(barrier, chips + jnp.minimum(zi, 1) + jnp.minimum(n_range - 1 - zi, 1))

    def to_left():
        return pltpu.make_async_remote_copy(
            src_ref=heads, dst_ref=right, send_sem=halo_send.at[0], recv_sem=halo_recv.at[0],
            device_id=dev(me, zi - 1), device_id_type=MESH_ID)

    def to_right():
        return pltpu.make_async_remote_copy(
            src_ref=tails, dst_ref=left, send_sem=halo_send.at[1], recv_sem=halo_recv.at[1],
            device_id=dev(me, zi + 1), device_id_type=MESH_ID)

    @pl.when(has_left)
    def _():
        to_left().start()

    @pl.when(has_right)
    def _():
        to_right().start()

    for load in loads[3:5]:
        load.wait()
    lane = lax.broadcasted_iota(jnp.int32, (LANES, LANES), 1).astype(F32)
    start = (zi * (blocks * LANES)).astype(F32)
    shift_values = shift_row[...].astype(F32)
    step = slopes[...] * float(LANES)
    step_re, step_im = jnp.cos(step), jnp.sin(step)
    for h in range(pulses // LANES):
        span = slice(h * LANES, (h + 1) * LANES)

        def column(row):
            return jnp.transpose(jnp.broadcast_to(row[:, span], (LANES, LANES)))

        phase = column(angles[...]) + column(slopes[...]) * (start + lane)
        e_re[span, :] = jnp.cos(phase)
        e_im[span, :] = jnp.sin(phase)
        d_re[span, :] = column(step_re)
        d_im[span, :] = column(step_im)
        reach[span, :] = column(shift_values) + lane + float(LANES - TAPS // 2 + 1)

    @pl.when(has_left)
    def _():
        to_right().wait_recv()

    @pl.when(has_right)
    def _():
        to_left().wait_recv()

    @pl.when(jnp.logical_not(has_left))
    def _():
        left[...] = jnp.zeros(left.shape, BF16)

    @pl.when(jnp.logical_not(has_right))
    def _():
        right[...] = jnp.zeros(right.shape, BF16)

    left_f[...] = left[...].astype(F32)
    right_f[...] = right[...].astype(F32)
    for load in loads[5:7]:
        load.wait()

    def x_copy(d, s):
        peer = ((chip + d) % chips) * 2 + core
        return pltpu.make_async_remote_copy(
            src_ref=sent.at[s], dst_ref=gathered.at[me, s],
            send_sem=x_send.at[d - 1, s], recv_sem=x_recv.at[d - 1, s],
            device_id=dev(peer, zi), device_id_type=MESH_ID)

    def sib_copy(s):
        return pltpu.make_async_remote_copy(
            src_ref=sent.at[s], dst_ref=gathered.at[me, s],
            send_sem=sib_send.at[s], recv_sem=sib_recv.at[s],
            device_id=dev(sibling, zi), device_id_type=MESH_ID)

    def fwd_copy(d, s):
        owner = ((chip + chips - d) % chips) * 2 + core
        return pltpu.make_async_remote_copy(
            src_ref=gathered.at[owner, s], dst_ref=gathered.at[owner, s],
            send_sem=fwd_send.at[d - 1, s], recv_sem=fwd_recv.at[d - 1, s],
            device_id=dev(sibling, zi), device_id_type=MESH_ID)

    def own_copy(s):
        return pltpu.make_async_copy(sent.at[s], gathered.at[me, s], own_sem.at[s])

    def forward(s):
        for d in range(1, chips):
            x_copy(d, s).wait_recv()
            fwd_copy(d, s).start()

    own_rows = 2 * blocks

    def one_sub(s, carry):
        def some_pulses(group, inner):
            for u in range(UNROLL):
                j = group * UNROLL + u
                pulse = s * SUB + j
                amount = (LANES - (shifts[0, pulse] + (LANES - TAPS // 2 + 1))) & (LANES - 1)
                rolled[pl.ds(j, own_rows, SUB), :] = pltpu.roll(cells[pulse].astype(F32), amount, axis=1)
                rolled[pl.ds(own_rows * SUB + j, 2, SUB), :] = pltpu.roll(left_f[pl.ds(2 * pulse, 2), :], amount, axis=1)
                rolled[pl.ds((own_rows + 2) * SUB + j, 2, SUB), :] = pltpu.roll(right_f[pl.ds(2 * pulse, 2), :], amount, axis=1)
            return inner

        lax.fori_loop(0, SUB // UNROLL, some_pulses, 0)

        rows = pl.ds(pl.multiple_of(s * SUB, SUB), SUB)
        at = reach[rows, :]
        first = at < float(LANES)
        second = at < float(2 * LANES)
        turn_re, turn_im = d_re[rows, :], d_im[rows, :]
        now_re, now_im = e_re[rows, :], e_im[rows, :]

        def block(b, c):
            b = min(b, blocks + 1)
            where = own_rows if b == 0 else own_rows + 2 if b == blocks + 1 else 2 * (b - 1)
            return rolled[(where + c) * SUB:(where + c + 1) * SUB, :]

        for b in range(blocks + 1):
            z = [
                jnp.where(first, block(b, c), jnp.where(second, block(b + 1, c), block(b + 2, c)))
                for c in range(2)
            ]
            span = slice(b * LANES, (b + 1) * LANES)
            y[0:SUB, span] = (now_re * z[0] - now_im * z[1]).astype(BF16)
            y[SUB:2 * SUB, span] = (now_im * z[0] + now_re * z[1]).astype(BF16)
            now_re, now_im = now_re * turn_re - now_im * turn_im, now_im * turn_re + now_re * turn_im

        taps_out[...] = jnp.dot(lhs[s], y[...], preferred_element_type=F32)
        width = (blocks + 1) * LANES
        total = taps_out[0:2 * BEAMS, :]
        for k in range(1, TAPS):
            total = total + pltpu.roll(taps_out[k * 2 * BEAMS:(k + 1) * 2 * BEAMS, :], width - k, axis=1)
        sent[s] = total[:, :blocks * LANES].astype(BF16)

        for d in range(1, chips):
            x_copy(d, s).start()
        sib_copy(s).start()
        own_copy(s).start()

        @pl.when(s >= 2)
        def _():
            forward(s - 2)

        return carry

    lax.fori_loop(0, subs, one_sub, 0)
    forward(subs - 2)

    n_rows = n_pulse * subs * 2 * BEAMS
    row = lax.broadcasted_iota(jnp.int32, (n_rows, FOOT), 0)
    beam = (row // (2 * BEAMS)) * BEAMS + row % BEAMS
    is_im = (row // BEAMS) % 2
    for load in loads[7:]:
        load.wait()
    for t in range(TILE_DEV):
        ids = footprint[pl.ds(me * TILE_DEV + t, 1), :]
        hit = beam == ids
        hot_re = jnp.where(hit & (is_im == 0), 1.0, 0.0).astype(BF16)
        hot_im = jnp.where(hit & (is_im == 1), 1.0, 0.0).astype(BF16)
        c_re = jnp.transpose(coeffs[t, 0].astype(F32)).astype(BF16)
        c_im = jnp.transpose(coeffs[t, 1].astype(F32)).astype(BF16)

        def spread(a, b):
            return lax.dot_general(a, b, (((1,), (1,)), ((), ())), preferred_element_type=F32)

        dense[t * 2 * AZ:t * 2 * AZ + AZ, :] = (spread(c_re, hot_re) - spread(c_im, hot_im)).astype(BF16)
        dense[t * 2 * AZ + AZ:(t + 1) * 2 * AZ, :] = (spread(c_im, hot_re) + spread(c_re, hot_im)).astype(BF16)

    forward(subs - 1)

    def finish(s, carry):
        own_copy(s).wait()
        sib_copy(s).wait()
        for d in range(1, chips):
            x_copy(d, s).wait_send()
            fwd_copy(d, s).wait()
        return carry

    lax.fori_loop(0, subs, finish, 0)

    @pl.when(has_left)
    def _():
        to_left().wait_send()

    @pl.when(has_right)
    def _():
        to_right().wait_send()


def project_kernel(dense, beams, out):
    out[...] = jnp.dot(dense[...], beams[...], preferred_element_type=F32).astype(BF16)


def body(n_pulse, n_range, echoes, shifts, tap_weights, angles, slopes, steering, footprint, tile_coeffs):
    pulses, _, width = echoes.shape
    blocks = width // LANES
    subs = pulses // SUB
    chips = n_pulse // 2
    by_block = echoes.reshape(pulses, 2, blocks, LANES).transpose(0, 2, 1, 3).reshape(pulses, 2 * blocks, LANES)
    heads = echoes[:, :, :LANES].reshape(2 * pulses, LANES)
    tails = echoes[:, :, width - LANES:].reshape(2 * pulses, LANES)
    n_rows = n_pulse * subs * 2 * BEAMS
    out_rows = TILE_DEV * 2 * AZ
    vmem = pl.BlockSpec(memory_space=pltpu.VMEM)
    hbm = pl.BlockSpec(memory_space=pltpu.HBM)
    anywhere = pl.BlockSpec(memory_space=pl.ANY)
    dma = pltpu.SemaphoreType.DMA
    gathered, dense = pl.pallas_call(
        functools.partial(beam_kernel, n_pulse, n_range, blocks, subs),
        out_shape=(
            jax.ShapeDtypeStruct((n_pulse, subs, 2 * BEAMS, width), BF16),
            jax.ShapeDtypeStruct((out_rows, n_rows), BF16),
        ),
        in_specs=[hbm] * 8 + [vmem] * 2,
        out_specs=(anywhere, vmem),
        scratch_shapes=[
            pltpu.VMEM((pulses, 2 * blocks, LANES), BF16),
            pltpu.SMEM((1, pulses), jnp.int32),
            pltpu.VMEM((1, pulses), jnp.int32),
            pltpu.VMEM((TAPS, pulses), F32),
            pltpu.VMEM((1, pulses), F32),
            pltpu.VMEM((1, pulses), F32),
            pltpu.VMEM((2 * BEAMS, SUB), BF16),
            pltpu.VMEM(footprint.shape, jnp.int32),
            pltpu.VMEM((TILE_DEV, 2, FOOT, AZ), BF16),
            pltpu.VMEM((2 * pulses, LANES), BF16),
            pltpu.VMEM((2 * pulses, LANES), BF16),
            pltpu.VMEM((2 * pulses, LANES), F32),
            pltpu.VMEM((2 * pulses, LANES), F32),
            pltpu.VMEM(((2 * blocks + 4) * SUB, LANES), F32),
            pltpu.VMEM((2 * SUB, width + LANES), BF16),
            pltpu.VMEM((TAPS * 2 * BEAMS, width + LANES), F32),
            pltpu.VMEM((subs, 2 * BEAMS, width), BF16),
            pltpu.VMEM((subs, TAPS * 2 * BEAMS, 2 * SUB), BF16),
            pltpu.VMEM((pulses, LANES), F32),
            pltpu.VMEM((pulses, LANES), F32),
            pltpu.VMEM((pulses, LANES), F32),
            pltpu.VMEM((pulses, LANES), F32),
            pltpu.VMEM((pulses, LANES), F32),
            dma((9,)),
            dma((2,)),
            dma((2,)),
            dma((subs,)),
            dma((chips - 1, subs)),
            dma((chips - 1, subs)),
            dma((subs,)),
            dma((subs,)),
            dma((chips - 1, subs)),
            dma((chips - 1, subs)),
        ],
        compiler_params=pltpu.CompilerParams(
            collective_id=0, has_side_effects=True, vmem_limit_bytes=63 * 1024 * 1024
        ),
    )(
        by_block, shifts[None], tap_weights.T, angles[None], slopes[None], steering.reshape(2 * BEAMS, SUB),
        footprint, tile_coeffs.transpose(0, 1, 3, 2), heads, tails,
    )

    columns = 512
    image = pl.pallas_call(
        project_kernel,
        grid=(width // columns,),
        out_shape=jax.ShapeDtypeStruct((out_rows, width), BF16),
        in_specs=[
            pl.BlockSpec((out_rows, n_rows), lambda i: (0, 0)),
            pl.BlockSpec((n_rows, columns), lambda i: (0, i)),
        ],
        out_specs=pl.BlockSpec((out_rows, columns), lambda i: (0, i)),
        compiler_params=pltpu.CompilerParams(vmem_limit_bytes=63 * 1024 * 1024),
    )(dense, gathered.reshape(n_rows, width))
    return image.reshape(TILE_DEV, 2, AZ, width)


def solution(mesh):
    placed = (
        P(("groups", "pulse"), None, "range"),
        P(("groups", "pulse")),
        P(("groups", "pulse"), None),
        P(("groups", "pulse")),
        P(("groups", "pulse")),
        P(),
        P("groups", None),
        P(("groups", "pulse"), None, None, None),
    )
    return jax.shard_map(
        functools.partial(body, mesh.shape["pulse"], mesh.shape["range"]),
        mesh=mesh,
        in_specs=placed,
        out_specs=P(("groups", "pulse"), None, None, "range"),
        check_vma=False,
    )
```

```python
import functools

import jax
import jax.numpy as jnp
from jax import lax
from jax.experimental import pallas as pl
from jax.experimental.pallas import tpu as pltpu
from jax.sharding import PartitionSpec as P

SUB = 32
BEAMS = 8
TAPS = 8
TILE_DEV = 4
FOOT = 32
AZ = 64
LANES = 128
F32 = jnp.float32
BF16 = jnp.bfloat16
MESH_ID = pl.DeviceIdType.MESH
UNROLL = 8


def beam_kernel(
    n_pulse, n_range, blocks, subs,
    echoes_in, shifts_in, taps_in, angles_in, slopes_in, steering_in, footprint_in, coeffs_in, heads, tails,
    gathered, dense,
    cells, shifts, shift_row, taps, angles, slopes, steering, footprint, coeffs,
    left, right, left_f, right_f, rolled, y, taps_out, sent,
    lhs, e_re, e_im, d_re, d_im, reach,
    load_sem, halo_send, halo_recv, own_sem,
    x_send, x_recv, sib_send, sib_recv, fwd_send, fwd_recv,
):
    chips = n_pulse // 2
    me = lax.axis_index("pulse")
    zi = lax.axis_index("range")
    gi = lax.axis_index("groups")
    chip = me // 2
    core = me % 2
    sibling = chip * 2 + (1 - core)
    pulses = subs * SUB
    has_left = zi > 0
    has_right = zi < n_range - 1

    def dev(p, z):
        return (gi, p, z)

    loads = [
        pltpu.make_async_copy(source, target, load_sem.at[n])
        for n, (source, target) in enumerate([
            (slopes_in, slopes), (taps_in, taps), (steering_in, steering), (angles_in, angles),
            (shifts_in, shift_row), (shifts_in, shifts), (echoes_in, cells),
            (footprint_in, footprint), (coeffs_in, coeffs),
        ])
    ]
    for load in loads:
        load.start()

    barrier = pltpu.get_barrier_semaphore()
    pl.semaphore_signal(barrier, inc=1, device_id=dev(sibling, zi), device_id_type=MESH_ID)
    for d in range(1, chips):
        peer = ((chip + d) % chips) * 2 + core
        pl.semaphore_signal(barrier, inc=1, device_id=dev(peer, zi), device_id_type=MESH_ID)

    @pl.when(has_left)
    def _():
        pl.semaphore_signal(barrier, inc=1, device_id=dev(me, zi - 1), device_id_type=MESH_ID)

    @pl.when(has_right)
    def _():
        pl.semaphore_signal(barrier, inc=1, device_id=dev(me, zi + 1), device_id_type=MESH_ID)

    pl.semaphore_wait(barrier, chips + jnp.minimum(zi, 1) + jnp.minimum(n_range - 1 - zi, 1))

    def to_left():
        return pltpu.make_async_remote_copy(
            src_ref=heads, dst_ref=right, send_sem=halo_send.at[0], recv_sem=halo_recv.at[0],
            device_id=dev(me, zi - 1), device_id_type=MESH_ID)

    def to_right():
        return pltpu.make_async_remote_copy(
            src_ref=tails, dst_ref=left, send_sem=halo_send.at[1], recv_sem=halo_recv.at[1],
            device_id=dev(me, zi + 1), device_id_type=MESH_ID)

    @pl.when(has_left)
    def _():
        to_left().start()

    @pl.when(has_right)
    def _():
        to_right().start()

    for load in loads[:3]:
        load.wait()
    tap_phase = slopes[...] * lax.broadcasted_iota(jnp.int32, (TAPS, pulses), 0).astype(F32)
    tap_re = taps[...] * jnp.cos(tap_phase)
    tap_im = -taps[...] * jnp.sin(tap_phase)
    weights = steering[...].astype(F32)
    st_re = jnp.concatenate([weights[0:BEAMS]] * subs, axis=1)
    st_im = jnp.concatenate([weights[BEAMS:2 * BEAMS]] * subs, axis=1)
    from_re, from_im = [], []
    for k in range(TAPS):
        w_re = st_re * tap_re[k:k + 1] - st_im * tap_im[k:k + 1]
        w_im = st_re * tap_im[k:k + 1] + st_im * tap_re[k:k + 1]
        from_re += [w_re, w_im]
        from_im += [-w_im, w_re]
    from_re = jnp.concatenate(from_re, axis=0)
    from_im = jnp.concatenate(from_im, axis=0)
    on_re = lax.broadcasted_iota(jnp.int32, (TAPS * 2 * BEAMS, LANES), 1) < SUB
    for s in range(subs):
        first = s * SUB // LANES * LANES
        off = s * SUB - first
        part_re = pltpu.roll(from_re[:, first:first + LANES], (LANES - off) % LANES, axis=1)
        part_im = pltpu.roll(from_im[:, first:first + LANES], (LANES + SUB - off) % LANES, axis=1)
        lhs[s] = jnp.where(on_re, part_re, part_im)[:, :2 * SUB].astype(BF16)

    for load in loads[3:5]:
        load.wait()
    lane = lax.broadcasted_iota(jnp.int32, (LANES, LANES), 1).astype(F32)
    start = (zi * (blocks * LANES)).astype(F32)
    shift_values = shift_row[...].astype(F32)
    step = slopes[...] * float(LANES)
    step_re, step_im = jnp.cos(step), jnp.sin(step)
    for h in range(pulses // LANES):
        span = slice(h * LANES, (h + 1) * LANES)

        def column(row):
            return jnp.transpose(jnp.broadcast_to(row[:, span], (LANES, LANES)))

        phase = column(angles[...]) + column(slopes[...]) * (start + lane)
        e_re[span, :] = jnp.cos(phase)
        e_im[span, :] = jnp.sin(phase)
        d_re[span, :] = column(step_re)
        d_im[span, :] = column(step_im)
        reach[span, :] = column(shift_values) + lane + float(LANES - TAPS // 2 + 1)

    @pl.when(has_left)
    def _():
        to_right().wait_recv()

    @pl.when(has_right)
    def _():
        to_left().wait_recv()

    @pl.when(jnp.logical_not(has_left))
    def _():
        left[...] = jnp.zeros(left.shape, BF16)

    @pl.when(jnp.logical_not(has_right))
    def _():
        right[...] = jnp.zeros(right.shape, BF16)

    left_f[...] = left[...].astype(F32)
    right_f[...] = right[...].astype(F32)
    for load in loads[5:7]:
        load.wait()

    def x_copy(d, s):
        peer = ((chip + d) % chips) * 2 + core
        return pltpu.make_async_remote_copy(
            src_ref=sent.at[s], dst_ref=gathered.at[me, s],
            send_sem=x_send.at[d - 1, s], recv_sem=x_recv.at[d - 1, s],
            device_id=dev(peer, zi), device_id_type=MESH_ID)

    def sib_copy(s):
        return pltpu.make_async_remote_copy(
            src_ref=sent.at[s], dst_ref=gathered.at[me, s],
            send_sem=sib_send.at[s], recv_sem=sib_recv.at[s],
            device_id=dev(sibling, zi), device_id_type=MESH_ID)

    def fwd_copy(d, s):
        owner = ((chip + chips - d) % chips) * 2 + core
        return pltpu.make_async_remote_copy(
            src_ref=gathered.at[owner, s], dst_ref=gathered.at[owner, s],
            send_sem=fwd_send.at[d - 1, s], recv_sem=fwd_recv.at[d - 1, s],
            device_id=dev(sibling, zi), device_id_type=MESH_ID)

    def own_copy(s):
        return pltpu.make_async_copy(sent.at[s], gathered.at[me, s], own_sem.at[s])

    def forward(s):
        for d in range(1, chips):
            x_copy(d, s).wait_recv()
            fwd_copy(d, s).start()

    own_rows = 2 * blocks

    def one_sub(s, carry):
        def some_pulses(group, inner):
            turned = []
            for u in range(UNROLL):
                pulse = s * SUB + group * UNROLL + u
                amount = (LANES - (shifts[0, pulse] + (LANES - TAPS // 2 + 1))) & (LANES - 1)
                turned.append([
                    pltpu.roll(part, amount, axis=1)
                    for part in (
                        cells[pulse].astype(F32), left_f[pl.ds(2 * pulse, 2), :], right_f[pl.ds(2 * pulse, 2), :],
                    )
                ])
            for u in range(UNROLL):
                j = group * UNROLL + u
                rolled[pl.ds(j, own_rows, SUB), :] = turned[u][0]
                rolled[pl.ds(own_rows * SUB + j, 2, SUB), :] = turned[u][1]
                rolled[pl.ds((own_rows + 2) * SUB + j, 2, SUB), :] = turned[u][2]
            return inner

        lax.fori_loop(0, SUB // UNROLL, some_pulses, 0)

        rows = pl.ds(pl.multiple_of(s * SUB, SUB), SUB)
        at = reach[rows, :]
        first = at < float(LANES)
        second = at < float(2 * LANES)
        turn_re, turn_im = d_re[rows, :], d_im[rows, :]
        now_re, now_im = e_re[rows, :], e_im[rows, :]

        def block(b, c):
            b = min(b, blocks + 1)
            where = own_rows if b == 0 else own_rows + 2 if b == blocks + 1 else 2 * (b - 1)
            return rolled[(where + c) * SUB:(where + c + 1) * SUB, :]

        for b in range(blocks + 1):
            z = [
                jnp.where(first, block(b, c), jnp.where(second, block(b + 1, c), block(b + 2, c)))
                for c in range(2)
            ]
            span = slice(b * LANES, (b + 1) * LANES)
            y[0:SUB, span] = (now_re * z[0] - now_im * z[1]).astype(BF16)
            y[SUB:2 * SUB, span] = (now_im * z[0] + now_re * z[1]).astype(BF16)
            now_re, now_im = now_re * turn_re - now_im * turn_im, now_im * turn_re + now_re * turn_im

        taps_out[...] = jnp.dot(lhs[s], y[...], preferred_element_type=F32)
        width = (blocks + 1) * LANES
        total = taps_out[0:2 * BEAMS, :]
        for k in range(1, TAPS):
            total = total + pltpu.roll(taps_out[k * 2 * BEAMS:(k + 1) * 2 * BEAMS, :], width - k, axis=1)
        sent[s] = total[:, :blocks * LANES].astype(BF16)

        for d in range(1, chips):
            x_copy(d, s).start()
        sib_copy(s).start()
        own_copy(s).start()

        @pl.when(s >= 2)
        def _():
            forward(s - 2)

        return carry

    lax.fori_loop(0, subs, one_sub, 0)
    forward(subs - 2)

    n_rows = n_pulse * subs * 2 * BEAMS
    row = lax.broadcasted_iota(jnp.int32, (n_rows, FOOT), 0)
    beam = (row // (2 * BEAMS)) * BEAMS + row % BEAMS
    is_im = (row // BEAMS) % 2
    for load in loads[7:]:
        load.wait()
    for t in range(TILE_DEV):
        ids = footprint[pl.ds(me * TILE_DEV + t, 1), :]
        hit = beam == ids
        hot_re = jnp.where(hit & (is_im == 0), 1.0, 0.0).astype(BF16)
        hot_im = jnp.where(hit & (is_im == 1), 1.0, 0.0).astype(BF16)
        c_re = jnp.transpose(coeffs[t, 0].astype(F32)).astype(BF16)
        c_im = jnp.transpose(coeffs[t, 1].astype(F32)).astype(BF16)

        def spread(a, b):
            return lax.dot_general(a, b, (((1,), (1,)), ((), ())), preferred_element_type=F32)

        dense[t * 2 * AZ:t * 2 * AZ + AZ, :] = (spread(c_re, hot_re) - spread(c_im, hot_im)).astype(BF16)
        dense[t * 2 * AZ + AZ:(t + 1) * 2 * AZ, :] = (spread(c_im, hot_re) + spread(c_re, hot_im)).astype(BF16)

    forward(subs - 1)

    def finish(s, carry):
        own_copy(s).wait()
        sib_copy(s).wait()
        for d in range(1, chips):
            x_copy(d, s).wait_send()
            fwd_copy(d, s).wait()
        return carry

    lax.fori_loop(0, subs, finish, 0)

    @pl.when(has_left)
    def _():
        to_left().wait_send()

    @pl.when(has_right)
    def _():
        to_right().wait_send()


def project_kernel(dense, beams, out):
    out[...] = jnp.dot(dense[...], beams[...], preferred_element_type=F32).astype(BF16)


def body(n_pulse, n_range, echoes, shifts, tap_weights, angles, slopes, steering, footprint, tile_coeffs):
    pulses, _, width = echoes.shape
    blocks = width // LANES
    subs = pulses // SUB
    chips = n_pulse // 2
    by_block = echoes.reshape(pulses, 2, blocks, LANES).transpose(0, 2, 1, 3).reshape(pulses, 2 * blocks, LANES)
    heads = echoes[:, :, :LANES].reshape(2 * pulses, LANES)
    tails = echoes[:, :, width - LANES:].reshape(2 * pulses, LANES)
    n_rows = n_pulse * subs * 2 * BEAMS
    out_rows = TILE_DEV * 2 * AZ
    vmem = pl.BlockSpec(memory_space=pltpu.VMEM)
    hbm = pl.BlockSpec(memory_space=pltpu.HBM)
    anywhere = pl.BlockSpec(memory_space=pl.ANY)
    dma = pltpu.SemaphoreType.DMA
    gathered, dense = pl.pallas_call(
        functools.partial(beam_kernel, n_pulse, n_range, blocks, subs),
        out_shape=(
            jax.ShapeDtypeStruct((n_pulse, subs, 2 * BEAMS, width), BF16),
            jax.ShapeDtypeStruct((out_rows, n_rows), BF16),
        ),
        in_specs=[hbm] * 8 + [vmem] * 2,
        out_specs=(anywhere, vmem),
        scratch_shapes=[
            pltpu.VMEM((pulses, 2 * blocks, LANES), BF16),
            pltpu.SMEM((1, pulses), jnp.int32),
            pltpu.VMEM((1, pulses), jnp.int32),
            pltpu.VMEM((TAPS, pulses), F32),
            pltpu.VMEM((1, pulses), F32),
            pltpu.VMEM((1, pulses), F32),
            pltpu.VMEM((2 * BEAMS, SUB), BF16),
            pltpu.VMEM(footprint.shape, jnp.int32),
            pltpu.VMEM((TILE_DEV, 2, FOOT, AZ), BF16),
            pltpu.VMEM((2 * pulses, LANES), BF16),
            pltpu.VMEM((2 * pulses, LANES), BF16),
            pltpu.VMEM((2 * pulses, LANES), F32),
            pltpu.VMEM((2 * pulses, LANES), F32),
            pltpu.VMEM(((2 * blocks + 4) * SUB, LANES), F32),
            pltpu.VMEM((2 * SUB, width + LANES), BF16),
            pltpu.VMEM((TAPS * 2 * BEAMS, width + LANES), F32),
            pltpu.VMEM((subs, 2 * BEAMS, width), BF16),
            pltpu.VMEM((subs, TAPS * 2 * BEAMS, 2 * SUB), BF16),
            pltpu.VMEM((pulses, LANES), F32),
            pltpu.VMEM((pulses, LANES), F32),
            pltpu.VMEM((pulses, LANES), F32),
            pltpu.VMEM((pulses, LANES), F32),
            pltpu.VMEM((pulses, LANES), F32),
            dma((9,)),
            dma((2,)),
            dma((2,)),
            dma((subs,)),
            dma((chips - 1, subs)),
            dma((chips - 1, subs)),
            dma((subs,)),
            dma((subs,)),
            dma((chips - 1, subs)),
            dma((chips - 1, subs)),
        ],
        compiler_params=pltpu.CompilerParams(
            collective_id=0, has_side_effects=True, vmem_limit_bytes=63 * 1024 * 1024
        ),
    )(
        by_block, shifts[None], tap_weights.T, angles[None], slopes[None], steering.reshape(2 * BEAMS, SUB),
        footprint, tile_coeffs.transpose(0, 1, 3, 2), heads, tails,
    )

    columns = 512
    image = pl.pallas_call(
        project_kernel,
        grid=(width // columns,),
        out_shape=jax.ShapeDtypeStruct((out_rows, width), BF16),
        in_specs=[
            pl.BlockSpec((out_rows, n_rows), lambda i: (0, 0)),
            pl.BlockSpec((n_rows, columns), lambda i: (0, i)),
        ],
        out_specs=pl.BlockSpec((out_rows, columns), lambda i: (0, i)),
        compiler_params=pltpu.CompilerParams(vmem_limit_bytes=63 * 1024 * 1024),
    )(dense, gathered.reshape(n_rows, width))
    return image.reshape(TILE_DEV, 2, AZ, width)


def solution(mesh):
    placed = (
        P(("groups", "pulse"), None, "range"),
        P(("groups", "pulse")),
        P(("groups", "pulse"), None),
        P(("groups", "pulse")),
        P(("groups", "pulse")),
        P(),
        P("groups", None),
        P(("groups", "pulse"), None, None, None),
    )
    return jax.shard_map(
        functools.partial(body, mesh.shape["pulse"], mesh.shape["range"]),
        mesh=mesh,
        in_specs=placed,
        out_specs=P(("groups", "pulse"), None, None, "range"),
        check_vma=False,
    )
```

```python
import functools

import jax
import jax.numpy as jnp
from jax import lax
from jax.experimental import pallas as pl
from jax.experimental.pallas import tpu as pltpu
from jax.sharding import PartitionSpec as P

SUB = 32
BEAMS = 8
TAPS = 8
TILE_DEV = 4
FOOT = 32
AZ = 64
LANES = 128
F32 = jnp.float32
BF16 = jnp.bfloat16
MESH_ID = pl.DeviceIdType.MESH
UNROLL = 8
LAG = 4


def beam_kernel(
    n_pulse, n_range, blocks, subs,
    echoes_in, shifts_in, taps_in, angles_in, slopes_in, steering_in, footprint_in, coeffs_in, heads, tails,
    gathered, dense,
    cells, shifts, shift_row, taps, angles, slopes, steering, footprint, coeffs,
    left, right, left_f, right_f, rolled, y, taps_out, sent,
    lhs, e_re, e_im, d_re, d_im, reach,
    load_sem, halo_send, halo_recv, own_sem,
    x_send, x_recv, sib_send, sib_recv, fwd_send, fwd_recv,
):
    chips = n_pulse // 2
    me = lax.axis_index("pulse")
    zi = lax.axis_index("range")
    gi = lax.axis_index("groups")
    chip = me // 2
    core = me % 2
    sibling = chip * 2 + (1 - core)
    pulses = subs * SUB
    has_left = zi > 0
    has_right = zi < n_range - 1

    def dev(p, z):
        return (gi, p, z)

    loads = [
        pltpu.make_async_copy(source, target, load_sem.at[n])
        for n, (source, target) in enumerate([
            (slopes_in, slopes), (taps_in, taps), (steering_in, steering), (angles_in, angles),
            (shifts_in, shift_row), (shifts_in, shifts), (echoes_in, cells),
            (footprint_in, footprint), (coeffs_in, coeffs),
        ])
    ]
    for load in loads:
        load.start()

    barrier = pltpu.get_barrier_semaphore()
    pl.semaphore_signal(barrier, inc=1, device_id=dev(sibling, zi), device_id_type=MESH_ID)
    for d in range(1, chips):
        peer = ((chip + d) % chips) * 2 + core
        pl.semaphore_signal(barrier, inc=1, device_id=dev(peer, zi), device_id_type=MESH_ID)

    @pl.when(has_left)
    def _():
        pl.semaphore_signal(barrier, inc=1, device_id=dev(me, zi - 1), device_id_type=MESH_ID)

    @pl.when(has_right)
    def _():
        pl.semaphore_signal(barrier, inc=1, device_id=dev(me, zi + 1), device_id_type=MESH_ID)

    pl.semaphore_wait(barrier, chips + jnp.minimum(zi, 1) + jnp.minimum(n_range - 1 - zi, 1))

    def to_left():
        return pltpu.make_async_remote_copy(
            src_ref=heads, dst_ref=right, send_sem=halo_send.at[0], recv_sem=halo_recv.at[0],
            device_id=dev(me, zi - 1), device_id_type=MESH_ID)

    def to_right():
        return pltpu.make_async_remote_copy(
            src_ref=tails, dst_ref=left, send_sem=halo_send.at[1], recv_sem=halo_recv.at[1],
            device_id=dev(me, zi + 1), device_id_type=MESH_ID)

    @pl.when(has_left)
    def _():
        to_left().start()

    @pl.when(has_right)
    def _():
        to_right().start()

    for load in loads[:3]:
        load.wait()
    tap_phase = slopes[...] * lax.broadcasted_iota(jnp.int32, (TAPS, pulses), 0).astype(F32)
    tap_re = taps[...] * jnp.cos(tap_phase)
    tap_im = -taps[...] * jnp.sin(tap_phase)
    weights = steering[...].astype(F32)
    st_re = jnp.concatenate([weights[0:BEAMS]] * subs, axis=1)
    st_im = jnp.concatenate([weights[BEAMS:2 * BEAMS]] * subs, axis=1)
    from_re, from_im = [], []
    for k in range(TAPS):
        w_re = st_re * tap_re[k:k + 1] - st_im * tap_im[k:k + 1]
        w_im = st_re * tap_im[k:k + 1] + st_im * tap_re[k:k + 1]
        from_re += [w_re, w_im]
        from_im += [-w_im, w_re]
    from_re = jnp.concatenate(from_re, axis=0)
    from_im = jnp.concatenate(from_im, axis=0)
    on_re = lax.broadcasted_iota(jnp.int32, (TAPS * 2 * BEAMS, LANES), 1) < SUB
    for s in range(subs):
        first = s * SUB // LANES * LANES
        off = s * SUB - first
        part_re = pltpu.roll(from_re[:, first:first + LANES], (LANES - off) % LANES, axis=1)
        part_im = pltpu.roll(from_im[:, first:first + LANES], (LANES + SUB - off) % LANES, axis=1)
        lhs[s] = jnp.where(on_re, part_re, part_im)[:, :2 * SUB].astype(BF16)

    for load in loads[3:5]:
        load.wait()
    lane = lax.broadcasted_iota(jnp.int32, (LANES, LANES), 1).astype(F32)
    start = (zi * (blocks * LANES)).astype(F32)
    shift_values = shift_row[...].astype(F32)
    step = slopes[...] * float(LANES)
    step_re, step_im = jnp.cos(step), jnp.sin(step)
    for h in range(pulses // LANES):
        span = slice(h * LANES, (h + 1) * LANES)

        def column(row):
            return jnp.transpose(jnp.broadcast_to(row[:, span], (LANES, LANES)))

        phase = column(angles[...]) + column(slopes[...]) * (start + lane)
        e_re[span, :] = jnp.cos(phase)
        e_im[span, :] = jnp.sin(phase)
        d_re[span, :] = column(step_re)
        d_im[span, :] = column(step_im)
        reach[span, :] = column(shift_values) + lane + float(LANES - TAPS // 2 + 1)

    @pl.when(has_left)
    def _():
        to_right().wait_recv()

    @pl.when(has_right)
    def _():
        to_left().wait_recv()

    @pl.when(jnp.logical_not(has_left))
    def _():
        left[...] = jnp.zeros(left.shape, BF16)

    @pl.when(jnp.logical_not(has_right))
    def _():
        right[...] = jnp.zeros(right.shape, BF16)

    left_f[...] = left[...].astype(F32)
    right_f[...] = right[...].astype(F32)
    for load in loads[5:7]:
        load.wait()

    def x_copy(d, s):
        peer = ((chip + d) % chips) * 2 + core
        return pltpu.make_async_remote_copy(
            src_ref=sent.at[s], dst_ref=gathered.at[me, s],
            send_sem=x_send.at[d - 1, s], recv_sem=x_recv.at[d - 1, s],
            device_id=dev(peer, zi), device_id_type=MESH_ID)

    def sib_copy(s):
        return pltpu.make_async_remote_copy(
            src_ref=sent.at[s], dst_ref=gathered.at[me, s],
            send_sem=sib_send.at[s], recv_sem=sib_recv.at[s],
            device_id=dev(sibling, zi), device_id_type=MESH_ID)

    def fwd_copy(d, s):
        owner = ((chip + chips - d) % chips) * 2 + core
        return pltpu.make_async_remote_copy(
            src_ref=gathered.at[owner, s], dst_ref=gathered.at[owner, s],
            send_sem=fwd_send.at[d - 1, s], recv_sem=fwd_recv.at[d - 1, s],
            device_id=dev(sibling, zi), device_id_type=MESH_ID)

    def own_copy(s):
        return pltpu.make_async_copy(sent.at[s], gathered.at[me, s], own_sem.at[s])

    def forward(s):
        for d in range(1, chips):
            x_copy(d, s).wait_recv()
            fwd_copy(d, s).start()

    own_rows = 2 * blocks

    def one_sub(s, carry):
        def some_pulses(group, inner):
            turned = []
            for u in range(UNROLL):
                pulse = s * SUB + group * UNROLL + u
                amount = (LANES - (shifts[0, pulse] + (LANES - TAPS // 2 + 1))) & (LANES - 1)
                turned.append([
                    pltpu.roll(part, amount, axis=1)
                    for part in (
                        cells[pulse].astype(F32), left_f[pl.ds(2 * pulse, 2), :], right_f[pl.ds(2 * pulse, 2), :],
                    )
                ])
            for u in range(UNROLL):
                j = group * UNROLL + u
                rolled[pl.ds(j, own_rows, SUB), :] = turned[u][0]
                rolled[pl.ds(own_rows * SUB + j, 2, SUB), :] = turned[u][1]
                rolled[pl.ds((own_rows + 2) * SUB + j, 2, SUB), :] = turned[u][2]
            return inner

        lax.fori_loop(0, SUB // UNROLL, some_pulses, 0)

        rows = pl.ds(pl.multiple_of(s * SUB, SUB), SUB)
        at = reach[rows, :]
        first = at < float(LANES)
        second = at < float(2 * LANES)
        turn_re, turn_im = d_re[rows, :], d_im[rows, :]
        now_re, now_im = e_re[rows, :], e_im[rows, :]

        def block(b, c):
            b = min(b, blocks + 1)
            where = own_rows if b == 0 else own_rows + 2 if b == blocks + 1 else 2 * (b - 1)
            return rolled[(where + c) * SUB:(where + c + 1) * SUB, :]

        for b in range(blocks + 1):
            z = [
                jnp.where(first, block(b, c), jnp.where(second, block(b + 1, c), block(b + 2, c)))
                for c in range(2)
            ]
            span = slice(b * LANES, (b + 1) * LANES)
            y[0:SUB, span] = (now_re * z[0] - now_im * z[1]).astype(BF16)
            y[SUB:2 * SUB, span] = (now_im * z[0] + now_re * z[1]).astype(BF16)
            now_re, now_im = now_re * turn_re - now_im * turn_im, now_im * turn_re + now_re * turn_im

        taps_out[...] = jnp.dot(lhs[s], y[...], preferred_element_type=F32)
        width = (blocks + 1) * LANES
        total = taps_out[0:2 * BEAMS, :]
        for k in range(1, TAPS):
            total = total + pltpu.roll(taps_out[k * 2 * BEAMS:(k + 1) * 2 * BEAMS, :], width - k, axis=1)
        sent[s] = total[:, :blocks * LANES].astype(BF16)

        for d in range(1, chips):
            x_copy(d, s).start()
        sib_copy(s).start()
        own_copy(s).start()

        @pl.when(s >= LAG)
        def _():
            forward(s - LAG)

        return carry

    lax.fori_loop(0, subs, one_sub, 0)
    for s in range(subs - LAG, subs - 1):
        forward(s)

    n_rows = n_pulse * subs * 2 * BEAMS
    row = lax.broadcasted_iota(jnp.int32, (n_rows, FOOT), 0)
    beam = (row // (2 * BEAMS)) * BEAMS + row % BEAMS
    is_im = (row // BEAMS) % 2
    for load in loads[7:]:
        load.wait()
    for t in range(TILE_DEV):
        ids = footprint[pl.ds(me * TILE_DEV + t, 1), :]
        hit = beam == ids
        hot_re = jnp.where(hit & (is_im == 0), 1.0, 0.0).astype(BF16)
        hot_im = jnp.where(hit & (is_im == 1), 1.0, 0.0).astype(BF16)
        c_re = jnp.transpose(coeffs[t, 0].astype(F32)).astype(BF16)
        c_im = jnp.transpose(coeffs[t, 1].astype(F32)).astype(BF16)

        def spread(a, b):
            return lax.dot_general(a, b, (((1,), (1,)), ((), ())), preferred_element_type=F32)

        dense[t * 2 * AZ:t * 2 * AZ + AZ, :] = (spread(c_re, hot_re) - spread(c_im, hot_im)).astype(BF16)
        dense[t * 2 * AZ + AZ:(t + 1) * 2 * AZ, :] = (spread(c_im, hot_re) + spread(c_re, hot_im)).astype(BF16)

    forward(subs - 1)

    def finish(s, carry):
        own_copy(s).wait()
        sib_copy(s).wait()
        for d in range(1, chips):
            x_copy(d, s).wait_send()
            fwd_copy(d, s).wait()
        return carry

    lax.fori_loop(0, subs, finish, 0)

    @pl.when(has_left)
    def _():
        to_left().wait_send()

    @pl.when(has_right)
    def _():
        to_right().wait_send()


def project_kernel(dense, beams, out):
    out[...] = jnp.dot(dense[...], beams[...], preferred_element_type=F32).astype(BF16)


def body(n_pulse, n_range, echoes, shifts, tap_weights, angles, slopes, steering, footprint, tile_coeffs):
    pulses, _, width = echoes.shape
    blocks = width // LANES
    subs = pulses // SUB
    chips = n_pulse // 2
    by_block = echoes.reshape(pulses, 2, blocks, LANES).transpose(0, 2, 1, 3).reshape(pulses, 2 * blocks, LANES)
    heads = echoes[:, :, :LANES].reshape(2 * pulses, LANES)
    tails = echoes[:, :, width - LANES:].reshape(2 * pulses, LANES)
    n_rows = n_pulse * subs * 2 * BEAMS
    out_rows = TILE_DEV * 2 * AZ
    vmem = pl.BlockSpec(memory_space=pltpu.VMEM)
    hbm = pl.BlockSpec(memory_space=pltpu.HBM)
    anywhere = pl.BlockSpec(memory_space=pl.ANY)
    dma = pltpu.SemaphoreType.DMA
    gathered, dense = pl.pallas_call(
        functools.partial(beam_kernel, n_pulse, n_range, blocks, subs),
        out_shape=(
            jax.ShapeDtypeStruct((n_pulse, subs, 2 * BEAMS, width), BF16),
            jax.ShapeDtypeStruct((out_rows, n_rows), BF16),
        ),
        in_specs=[hbm] * 8 + [vmem] * 2,
        out_specs=(anywhere, vmem),
        scratch_shapes=[
            pltpu.VMEM((pulses, 2 * blocks, LANES), BF16),
            pltpu.SMEM((1, pulses), jnp.int32),
            pltpu.VMEM((1, pulses), jnp.int32),
            pltpu.VMEM((TAPS, pulses), F32),
            pltpu.VMEM((1, pulses), F32),
            pltpu.VMEM((1, pulses), F32),
            pltpu.VMEM((2 * BEAMS, SUB), BF16),
            pltpu.VMEM(footprint.shape, jnp.int32),
            pltpu.VMEM((TILE_DEV, 2, FOOT, AZ), BF16),
            pltpu.VMEM((2 * pulses, LANES), BF16),
            pltpu.VMEM((2 * pulses, LANES), BF16),
            pltpu.VMEM((2 * pulses, LANES), F32),
            pltpu.VMEM((2 * pulses, LANES), F32),
            pltpu.VMEM(((2 * blocks + 4) * SUB, LANES), F32),
            pltpu.VMEM((2 * SUB, width + LANES), BF16),
            pltpu.VMEM((TAPS * 2 * BEAMS, width + LANES), F32),
            pltpu.VMEM((subs, 2 * BEAMS, width), BF16),
            pltpu.VMEM((subs, TAPS * 2 * BEAMS, 2 * SUB), BF16),
            pltpu.VMEM((pulses, LANES), F32),
            pltpu.VMEM((pulses, LANES), F32),
            pltpu.VMEM((pulses, LANES), F32),
            pltpu.VMEM((pulses, LANES), F32),
            pltpu.VMEM((pulses, LANES), F32),
            dma((9,)),
            dma((2,)),
            dma((2,)),
            dma((subs,)),
            dma((chips - 1, subs)),
            dma((chips - 1, subs)),
            dma((subs,)),
            dma((subs,)),
            dma((chips - 1, subs)),
            dma((chips - 1, subs)),
        ],
        compiler_params=pltpu.CompilerParams(
            collective_id=0, has_side_effects=True, vmem_limit_bytes=63 * 1024 * 1024
        ),
    )(
        by_block, shifts[None], tap_weights.T, angles[None], slopes[None], steering.reshape(2 * BEAMS, SUB),
        footprint, tile_coeffs.transpose(0, 1, 3, 2), heads, tails,
    )

    columns = 512
    image = pl.pallas_call(
        project_kernel,
        grid=(width // columns,),
        out_shape=jax.ShapeDtypeStruct((out_rows, width), BF16),
        in_specs=[
            pl.BlockSpec((out_rows, n_rows), lambda i: (0, 0)),
            pl.BlockSpec((n_rows, columns), lambda i: (0, i)),
        ],
        out_specs=pl.BlockSpec((out_rows, columns), lambda i: (0, i)),
        compiler_params=pltpu.CompilerParams(vmem_limit_bytes=63 * 1024 * 1024),
    )(dense, gathered.reshape(n_rows, width))
    return image.reshape(TILE_DEV, 2, AZ, width)


def solution(mesh):
    placed = (
        P(("groups", "pulse"), None, "range"),
        P(("groups", "pulse")),
        P(("groups", "pulse"), None),
        P(("groups", "pulse")),
        P(("groups", "pulse")),
        P(),
        P("groups", None),
        P(("groups", "pulse"), None, None, None),
    )
    return jax.shard_map(
        functools.partial(body, mesh.shape["pulse"], mesh.shape["range"]),
        mesh=mesh,
        in_specs=placed,
        out_specs=P(("groups", "pulse"), None, None, "range"),
        check_vma=False,
    )
```

```python
import functools

import jax
import jax.numpy as jnp
from jax import lax
from jax.experimental import pallas as pl
from jax.experimental.pallas import tpu as pltpu
from jax.sharding import PartitionSpec as P

SUB = 32
BEAMS = 8
TAPS = 8
TILE_DEV = 4
FOOT = 32
AZ = 64
LANES = 128
F32 = jnp.float32
BF16 = jnp.bfloat16
MESH_ID = pl.DeviceIdType.MESH
UNROLL = 8
LAG = 4
COLUMNS = 256


def beam_kernel(
    n_pulse, n_range, blocks, subs,
    echoes_in, shifts_in, taps_in, angles_in, slopes_in, steering_in, footprint_in, coeffs_in, heads, tails,
    out,
    cells, shifts, shift_row, taps, angles, slopes, steering, footprint, coeffs,
    left, right, left_f, right_f, rolled, y, taps_out, gathered, dense, half_sum, image,
    lhs, e_re, e_im, d_re, d_im, reach,
    load_sem, halo_send, halo_recv, out_sem,
    x_send, x_recv, sib_send, sib_recv, fwd_send, fwd_recv,
):
    chips = n_pulse // 2
    me = lax.axis_index("pulse")
    zi = lax.axis_index("range")
    gi = lax.axis_index("groups")
    chip = me // 2
    core = me % 2
    sibling = chip * 2 + (1 - core)
    pulses = subs * SUB
    has_left = zi > 0
    has_right = zi < n_range - 1

    def dev(p, z):
        return (gi, p, z)

    loads = [
        pltpu.make_async_copy(source, target, load_sem.at[n])
        for n, (source, target) in enumerate([
            (slopes_in, slopes), (taps_in, taps), (steering_in, steering), (angles_in, angles),
            (shifts_in, shift_row), (shifts_in, shifts), (echoes_in, cells),
            (footprint_in, footprint), (coeffs_in, coeffs),
        ])
    ]
    for load in loads:
        load.start()

    barrier = pltpu.get_barrier_semaphore()
    pl.semaphore_signal(barrier, inc=1, device_id=dev(sibling, zi), device_id_type=MESH_ID)
    for d in range(1, chips):
        peer = ((chip + d) % chips) * 2 + core
        pl.semaphore_signal(barrier, inc=1, device_id=dev(peer, zi), device_id_type=MESH_ID)

    @pl.when(has_left)
    def _():
        pl.semaphore_signal(barrier, inc=1, device_id=dev(me, zi - 1), device_id_type=MESH_ID)

    @pl.when(has_right)
    def _():
        pl.semaphore_signal(barrier, inc=1, device_id=dev(me, zi + 1), device_id_type=MESH_ID)

    pl.semaphore_wait(barrier, chips + jnp.minimum(zi, 1) + jnp.minimum(n_range - 1 - zi, 1))

    def to_left():
        return pltpu.make_async_remote_copy(
            src_ref=heads, dst_ref=right, send_sem=halo_send.at[0], recv_sem=halo_recv.at[0],
            device_id=dev(me, zi - 1), device_id_type=MESH_ID)

    def to_right():
        return pltpu.make_async_remote_copy(
            src_ref=tails, dst_ref=left, send_sem=halo_send.at[1], recv_sem=halo_recv.at[1],
            device_id=dev(me, zi + 1), device_id_type=MESH_ID)

    @pl.when(has_left)
    def _():
        to_left().start()

    @pl.when(has_right)
    def _():
        to_right().start()

    for load in loads[:3]:
        load.wait()
    tap_phase = slopes[...] * lax.broadcasted_iota(jnp.int32, (TAPS, pulses), 0).astype(F32)
    tap_re = taps[...] * jnp.cos(tap_phase)
    tap_im = -taps[...] * jnp.sin(tap_phase)
    weights = steering[...].astype(F32)
    st_re = jnp.concatenate([weights[0:BEAMS]] * subs, axis=1)
    st_im = jnp.concatenate([weights[BEAMS:2 * BEAMS]] * subs, axis=1)
    from_re, from_im = [], []
    for k in range(TAPS):
        w_re = st_re * tap_re[k:k + 1] - st_im * tap_im[k:k + 1]
        w_im = st_re * tap_im[k:k + 1] + st_im * tap_re[k:k + 1]
        from_re += [w_re, w_im]
        from_im += [-w_im, w_re]
    from_re = jnp.concatenate(from_re, axis=0)
    from_im = jnp.concatenate(from_im, axis=0)
    on_re = lax.broadcasted_iota(jnp.int32, (TAPS * 2 * BEAMS, LANES), 1) < SUB
    for s in range(subs):
        first = s * SUB // LANES * LANES
        off = s * SUB - first
        part_re = pltpu.roll(from_re[:, first:first + LANES], (LANES - off) % LANES, axis=1)
        part_im = pltpu.roll(from_im[:, first:first + LANES], (LANES + SUB - off) % LANES, axis=1)
        lhs[s] = jnp.where(on_re, part_re, part_im)[:, :2 * SUB].astype(BF16)

    for load in loads[3:5]:
        load.wait()
    lane = lax.broadcasted_iota(jnp.int32, (LANES, LANES), 1).astype(F32)
    start = (zi * (blocks * LANES)).astype(F32)
    shift_values = shift_row[...].astype(F32)
    step = slopes[...] * float(LANES)
    step_re, step_im = jnp.cos(step), jnp.sin(step)
    for h in range(pulses // LANES):
        span = slice(h * LANES, (h + 1) * LANES)

        def column(row):
            return jnp.transpose(jnp.broadcast_to(row[:, span], (LANES, LANES)))

        phase = column(angles[...]) + column(slopes[...]) * (start + lane)
        e_re[span, :] = jnp.cos(phase)
        e_im[span, :] = jnp.sin(phase)
        d_re[span, :] = column(step_re)
        d_im[span, :] = column(step_im)
        reach[span, :] = column(shift_values) + lane + float(LANES - TAPS // 2 + 1)

    @pl.when(has_left)
    def _():
        to_right().wait_recv()

    @pl.when(has_right)
    def _():
        to_left().wait_recv()

    @pl.when(jnp.logical_not(has_left))
    def _():
        left[...] = jnp.zeros(left.shape, BF16)

    @pl.when(jnp.logical_not(has_right))
    def _():
        right[...] = jnp.zeros(right.shape, BF16)

    left_f[...] = left[...].astype(F32)
    right_f[...] = right[...].astype(F32)
    for load in loads[5:7]:
        load.wait()

    def slot(s, owner):
        return gathered.at[pl.ds(pl.multiple_of((s * n_pulse + owner) * 2 * BEAMS, 2 * BEAMS), 2 * BEAMS), :]

    def x_copy(d, s):
        peer = ((chip + d) % chips) * 2 + core
        return pltpu.make_async_remote_copy(
            src_ref=slot(s, me), dst_ref=slot(s, me),
            send_sem=x_send.at[d - 1, s], recv_sem=x_recv.at[d - 1, s],
            device_id=dev(peer, zi), device_id_type=MESH_ID)

    def sib_copy(s):
        return pltpu.make_async_remote_copy(
            src_ref=slot(s, me), dst_ref=slot(s, me),
            send_sem=sib_send.at[s], recv_sem=sib_recv.at[s],
            device_id=dev(sibling, zi), device_id_type=MESH_ID)

    def fwd_copy(d, s):
        owner = ((chip + chips - d) % chips) * 2 + core
        return pltpu.make_async_remote_copy(
            src_ref=slot(s, owner), dst_ref=slot(s, owner),
            send_sem=fwd_send.at[d - 1, s], recv_sem=fwd_recv.at[d - 1, s],
            device_id=dev(sibling, zi), device_id_type=MESH_ID)

    def forward(s):
        for d in range(1, chips):
            x_copy(d, s).wait_recv()
            fwd_copy(d, s).start()

    own_rows = 2 * blocks

    def one_sub(s, carry):
        def some_pulses(group, inner):
            turned = []
            for u in range(UNROLL):
                pulse = s * SUB + group * UNROLL + u
                amount = (LANES - (shifts[0, pulse] + (LANES - TAPS // 2 + 1))) & (LANES - 1)
                turned.append([
                    pltpu.roll(part, amount, axis=1)
                    for part in (
                        cells[pulse].astype(F32), left_f[pl.ds(2 * pulse, 2), :], right_f[pl.ds(2 * pulse, 2), :],
                    )
                ])
            for u in range(UNROLL):
                j = group * UNROLL + u
                rolled[pl.ds(j, own_rows, SUB), :] = turned[u][0]
                rolled[pl.ds(own_rows * SUB + j, 2, SUB), :] = turned[u][1]
                rolled[pl.ds((own_rows + 2) * SUB + j, 2, SUB), :] = turned[u][2]
            return inner

        lax.fori_loop(0, SUB // UNROLL, some_pulses, 0)

        rows = pl.ds(pl.multiple_of(s * SUB, SUB), SUB)
        at = reach[rows, :]
        first = at < float(LANES)
        second = at < float(2 * LANES)
        turn_re, turn_im = d_re[rows, :], d_im[rows, :]
        now_re, now_im = e_re[rows, :], e_im[rows, :]

        def block(b, c):
            b = min(b, blocks + 1)
            where = own_rows if b == 0 else own_rows + 2 if b == blocks + 1 else 2 * (b - 1)
            return rolled[(where + c) * SUB:(where + c + 1) * SUB, :]

        for b in range(blocks + 1):
            z = [
                jnp.where(first, block(b, c), jnp.where(second, block(b + 1, c), block(b + 2, c)))
                for c in range(2)
            ]
            span = slice(b * LANES, (b + 1) * LANES)
            y[0:SUB, span] = (now_re * z[0] - now_im * z[1]).astype(BF16)
            y[SUB:2 * SUB, span] = (now_im * z[0] + now_re * z[1]).astype(BF16)
            now_re, now_im = now_re * turn_re - now_im * turn_im, now_im * turn_re + now_re * turn_im

        taps_out[...] = jnp.dot(lhs[s], y[...], preferred_element_type=F32)
        width = (blocks + 1) * LANES
        total = taps_out[0:2 * BEAMS, :]
        for k in range(1, TAPS):
            total = total + pltpu.roll(taps_out[k * 2 * BEAMS:(k + 1) * 2 * BEAMS, :], width - k, axis=1)
        slot(s, me)[...] = total[:, :blocks * LANES].astype(BF16)

        for d in range(1, chips):
            x_copy(d, s).start()
        sib_copy(s).start()

        @pl.when(s >= LAG)
        def _():
            forward(s - LAG)

        return carry

    lax.fori_loop(0, subs, one_sub, 0)
    n_rows = n_pulse * subs * 2 * BEAMS
    row = lax.broadcasted_iota(jnp.int32, (n_rows, FOOT), 0)
    block_row = row // (2 * BEAMS)
    beam = ((block_row % n_pulse) * subs + block_row // n_pulse) * BEAMS + row % BEAMS
    is_im = (row // BEAMS) % 2
    for load in loads[7:]:
        load.wait()
    for t in range(TILE_DEV):
        ids = footprint[pl.ds(me * TILE_DEV + t, 1), :]
        hit = beam == ids
        hot_re = jnp.where(hit & (is_im == 0), 1.0, 0.0).astype(BF16)
        hot_im = jnp.where(hit & (is_im == 1), 1.0, 0.0).astype(BF16)
        c_re = jnp.transpose(coeffs[t, 0].astype(F32)).astype(BF16)
        c_im = jnp.transpose(coeffs[t, 1].astype(F32)).astype(BF16)

        def spread(a, b):
            return lax.dot_general(a, b, (((1,), (1,)), ((), ())), preferred_element_type=F32)

        dense[t * 2 * AZ:t * 2 * AZ + AZ, :] = (spread(c_re, hot_re) - spread(c_im, hot_im)).astype(BF16)
        dense[t * 2 * AZ + AZ:(t + 1) * 2 * AZ, :] = (spread(c_im, hot_re) + spread(c_re, hot_im)).astype(BF16)

    def landed(first, last):
        def one(s, carry):
            sib_copy(s).wait_recv()
            for d in range(1, chips):
                fwd_copy(d, s).wait_recv()
            return carry

        lax.fori_loop(first, last, one, 0)

    early = subs - LAG
    half = early * n_pulse * 2 * BEAMS
    pieces = blocks * LANES // COLUMNS

    def columns(n):
        return pl.ds(pl.multiple_of(n * COLUMNS, COLUMNS), COLUMNS)

    def first_half(n, carry):
        half_sum[:, columns(n)] = jnp.dot(
            dense[:, 0:half], gathered[0:half, columns(n)], preferred_element_type=F32)
        return carry

    def out_copy(n):
        return pltpu.make_async_copy(image.at[:, columns(n)], out.at[:, columns(n)], out_sem.at[n])

    def second_half(n, carry):
        image[:, columns(n)] = (half_sum[:, columns(n)] + jnp.dot(
            dense[:, half:n_rows], gathered[half:n_rows, columns(n)], preferred_element_type=F32)).astype(BF16)
        out_copy(n).start()
        return carry

    forward(early)
    landed(0, early)
    lax.fori_loop(0, pieces // 2, first_half, 0)
    forward(early + 1)
    lax.fori_loop(pieces // 2, pieces, first_half, 0)
    for s in range(early + 2, subs):
        forward(s)
    landed(early, subs)
    lax.fori_loop(0, pieces, second_half, 0)

    def finish(s, carry):
        sib_copy(s).wait_send()
        for d in range(1, chips):
            x_copy(d, s).wait_send()
            fwd_copy(d, s).wait_send()
        return carry

    lax.fori_loop(0, subs, finish, 0)

    def drain(n, carry):
        out_copy(n).wait()
        return carry

    lax.fori_loop(0, pieces, drain, 0)

    @pl.when(has_left)
    def _():
        to_left().wait_send()

    @pl.when(has_right)
    def _():
        to_right().wait_send()


def body(n_pulse, n_range, echoes, shifts, tap_weights, angles, slopes, steering, footprint, tile_coeffs):
    pulses, _, width = echoes.shape
    blocks = width // LANES
    subs = pulses // SUB
    chips = n_pulse // 2
    by_block = echoes.reshape(pulses, 2, blocks, LANES).transpose(0, 2, 1, 3).reshape(pulses, 2 * blocks, LANES)
    heads = echoes[:, :, :LANES].reshape(2 * pulses, LANES)
    tails = echoes[:, :, width - LANES:].reshape(2 * pulses, LANES)
    n_rows = n_pulse * subs * 2 * BEAMS
    out_rows = TILE_DEV * 2 * AZ
    vmem = pl.BlockSpec(memory_space=pltpu.VMEM)
    hbm = pl.BlockSpec(memory_space=pltpu.HBM)
    dma = pltpu.SemaphoreType.DMA
    image = pl.pallas_call(
        functools.partial(beam_kernel, n_pulse, n_range, blocks, subs),
        out_shape=jax.ShapeDtypeStruct((out_rows, width), BF16),
        in_specs=[hbm] * 8 + [vmem] * 2,
        out_specs=hbm,
        scratch_shapes=[
            pltpu.VMEM((pulses, 2 * blocks, LANES), BF16),
            pltpu.SMEM((1, pulses), jnp.int32),
            pltpu.VMEM((1, pulses), jnp.int32),
            pltpu.VMEM((TAPS, pulses), F32),
            pltpu.VMEM((1, pulses), F32),
            pltpu.VMEM((1, pulses), F32),
            pltpu.VMEM((2 * BEAMS, SUB), BF16),
            pltpu.VMEM(footprint.shape, jnp.int32),
            pltpu.VMEM((TILE_DEV, 2, FOOT, AZ), BF16),
            pltpu.VMEM((2 * pulses, LANES), BF16),
            pltpu.VMEM((2 * pulses, LANES), BF16),
            pltpu.VMEM((2 * pulses, LANES), F32),
            pltpu.VMEM((2 * pulses, LANES), F32),
            pltpu.VMEM(((2 * blocks + 4) * SUB, LANES), F32),
            pltpu.VMEM((2 * SUB, width + LANES), BF16),
            pltpu.VMEM((TAPS * 2 * BEAMS, width + LANES), F32),
            pltpu.VMEM((n_rows, width), BF16),
            pltpu.VMEM((out_rows, n_rows), BF16),
            pltpu.VMEM((out_rows, width), F32),
            pltpu.VMEM((out_rows, width), BF16),
            pltpu.VMEM((subs, TAPS * 2 * BEAMS, 2 * SUB), BF16),
            pltpu.VMEM((pulses, LANES), F32),
            pltpu.VMEM((pulses, LANES), F32),
            pltpu.VMEM((pulses, LANES), F32),
            pltpu.VMEM((pulses, LANES), F32),
            pltpu.VMEM((pulses, LANES), F32),
            dma((9,)),
            dma((2,)),
            dma((2,)),
            dma((width // COLUMNS,)),
            dma((chips - 1, subs)),
            dma((chips - 1, subs)),
            dma((subs,)),
            dma((subs,)),
            dma((chips - 1, subs)),
            dma((chips - 1, subs)),
        ],
        compiler_params=pltpu.CompilerParams(
            collective_id=0, has_side_effects=True, vmem_limit_bytes=63 * 1024 * 1024
        ),
    )(
        by_block, shifts[None], tap_weights.T, angles[None], slopes[None], steering.reshape(2 * BEAMS, SUB),
        footprint, tile_coeffs.transpose(0, 1, 3, 2), heads, tails,
    )
    return image.reshape(TILE_DEV, 2, AZ, width)


def solution(mesh):
    placed = (
        P(("groups", "pulse"), None, "range"),
        P(("groups", "pulse")),
        P(("groups", "pulse"), None),
        P(("groups", "pulse")),
        P(("groups", "pulse")),
        P(),
        P("groups", None),
        P(("groups", "pulse"), None, None, None),
    )
    return jax.shard_map(
        functools.partial(body, mesh.shape["pulse"], mesh.shape["range"]),
        mesh=mesh,
        in_specs=placed,
        out_specs=P(("groups", "pulse"), None, None, "range"),
        check_vma=False,
    )
```

```python
import functools

import jax
import jax.numpy as jnp
from jax import lax
from jax.experimental import pallas as pl
from jax.experimental.pallas import tpu as pltpu
from jax.sharding import PartitionSpec as P

SUB = 32
BEAMS = 8
TAPS = 8
TILE_DEV = 4
FOOT = 32
AZ = 64
LANES = 128
F32 = jnp.float32
BF16 = jnp.bfloat16
MESH_ID = pl.DeviceIdType.MESH
UNROLL = 8
LAG = 4
PITCH = SUB + 8
COPIES = 8
COLUMNS = 256


def beam_kernel(
    n_pulse, n_range, blocks, subs,
    echoes_in, shifts_in, taps_in, angles_in, slopes_in, steering_in, footprint_in, coeffs_in, heads, tails,
    out,
    cells, shifts, shift_row, taps, angles, slopes, steering, footprint, coeffs,
    left, right, left_f, right_f, rolled, y, taps_out, gathered, dense, half_sum, image,
    lhs, e_re, e_im, d_re, d_im, reach,
    load_sem, halo_send, halo_recv, out_sem,
    x_send, x_recv, sib_send, sib_recv, fwd_send, fwd_recv,
):
    chips = n_pulse // 2
    me = lax.axis_index("pulse")
    zi = lax.axis_index("range")
    gi = lax.axis_index("groups")
    chip = me // 2
    core = me % 2
    sibling = chip * 2 + (1 - core)
    pulses = subs * SUB
    has_left = zi > 0
    has_right = zi < n_range - 1

    def dev(p, z):
        return (gi, p, z)

    loads = [
        pltpu.make_async_copy(source, target, load_sem.at[n])
        for n, (source, target) in enumerate([
            (slopes_in, slopes), (taps_in, taps), (steering_in, steering), (angles_in, angles),
            (shifts_in, shift_row), (shifts_in, shifts), (echoes_in, cells),
            (footprint_in, footprint), (coeffs_in, coeffs),
        ])
    ]
    for load in loads:
        load.start()

    barrier = pltpu.get_barrier_semaphore()
    pl.semaphore_signal(barrier, inc=1, device_id=dev(sibling, zi), device_id_type=MESH_ID)
    for d in range(1, chips):
        peer = ((chip + d) % chips) * 2 + core
        pl.semaphore_signal(barrier, inc=1, device_id=dev(peer, zi), device_id_type=MESH_ID)

    @pl.when(has_left)
    def _():
        pl.semaphore_signal(barrier, inc=1, device_id=dev(me, zi - 1), device_id_type=MESH_ID)

    @pl.when(has_right)
    def _():
        pl.semaphore_signal(barrier, inc=1, device_id=dev(me, zi + 1), device_id_type=MESH_ID)

    pl.semaphore_wait(barrier, chips + jnp.minimum(zi, 1) + jnp.minimum(n_range - 1 - zi, 1))

    def to_left():
        return pltpu.make_async_remote_copy(
            src_ref=heads, dst_ref=right, send_sem=halo_send.at[0], recv_sem=halo_recv.at[0],
            device_id=dev(me, zi - 1), device_id_type=MESH_ID)

    def to_right():
        return pltpu.make_async_remote_copy(
            src_ref=tails, dst_ref=left, send_sem=halo_send.at[1], recv_sem=halo_recv.at[1],
            device_id=dev(me, zi + 1), device_id_type=MESH_ID)

    @pl.when(has_left)
    def _():
        to_left().start()

    @pl.when(has_right)
    def _():
        to_right().start()

    for load in loads[:3]:
        load.wait()
    tap_phase = slopes[...] * lax.broadcasted_iota(jnp.int32, (TAPS, pulses), 0).astype(F32)
    tap_re = taps[...] * jnp.cos(tap_phase)
    tap_im = -taps[...] * jnp.sin(tap_phase)
    weights = steering[...].astype(F32)
    st_re = jnp.concatenate([weights[0:BEAMS]] * subs, axis=1)
    st_im = jnp.concatenate([weights[BEAMS:2 * BEAMS]] * subs, axis=1)
    from_re, from_im = [], []
    for k in range(TAPS):
        w_re = st_re * tap_re[k:k + 1] - st_im * tap_im[k:k + 1]
        w_im = st_re * tap_im[k:k + 1] + st_im * tap_re[k:k + 1]
        from_re += [w_re, w_im]
        from_im += [-w_im, w_re]
    from_re = jnp.concatenate(from_re, axis=0)
    from_im = jnp.concatenate(from_im, axis=0)
    on_re = lax.broadcasted_iota(jnp.int32, (TAPS * 2 * BEAMS, LANES), 1) < SUB
    for s in range(subs):
        first = s * SUB // LANES * LANES
        off = s * SUB - first
        part_re = pltpu.roll(from_re[:, first:first + LANES], (LANES - off) % LANES, axis=1)
        part_im = pltpu.roll(from_im[:, first:first + LANES], (LANES + SUB - off) % LANES, axis=1)
        lhs[s] = jnp.where(on_re, part_re, part_im)[:, :2 * SUB].astype(BF16)

    for load in loads[3:5]:
        load.wait()
    lane = lax.broadcasted_iota(jnp.int32, (LANES, LANES), 1).astype(F32)
    start = (zi * (blocks * LANES)).astype(F32)
    shift_values = shift_row[...].astype(F32)
    step = slopes[...] * float(LANES)
    step_re, step_im = jnp.cos(step), jnp.sin(step)
    for h in range(pulses // LANES):
        span = slice(h * LANES, (h + 1) * LANES)

        def column(row):
            return jnp.transpose(jnp.broadcast_to(row[:, span], (LANES, LANES)))

        phase = column(angles[...]) + column(slopes[...]) * (start + lane)
        e_re[span, :] = jnp.cos(phase)
        e_im[span, :] = jnp.sin(phase)
        d_re[span, :] = column(step_re)
        d_im[span, :] = column(step_im)
        reach[span, :] = column(shift_values) + lane + float(LANES - TAPS // 2 + 1)

    @pl.when(has_left)
    def _():
        to_right().wait_recv()

    @pl.when(has_right)
    def _():
        to_left().wait_recv()

    @pl.when(jnp.logical_not(has_left))
    def _():
        left[...] = jnp.zeros(left.shape, BF16)

    @pl.when(jnp.logical_not(has_right))
    def _():
        right[...] = jnp.zeros(right.shape, BF16)

    left_f[...] = left[...].astype(F32)
    right_f[...] = right[...].astype(F32)
    for load in loads[5:7]:
        load.wait()

    def slot(s, owner):
        return gathered.at[pl.ds(pl.multiple_of((s * n_pulse + owner) * 2 * BEAMS, 2 * BEAMS), 2 * BEAMS), :]

    def x_copy(d, s):
        peer = ((chip + d) % chips) * 2 + core
        return pltpu.make_async_remote_copy(
            src_ref=slot(s, me), dst_ref=slot(s, me),
            send_sem=x_send.at[d - 1, s], recv_sem=x_recv.at[d - 1, s],
            device_id=dev(peer, zi), device_id_type=MESH_ID)

    def sib_copy(s):
        return pltpu.make_async_remote_copy(
            src_ref=slot(s, me), dst_ref=slot(s, me),
            send_sem=sib_send.at[s], recv_sem=sib_recv.at[s],
            device_id=dev(sibling, zi), device_id_type=MESH_ID)

    def fwd_copy(d, s):
        owner = ((chip + chips - d) % chips) * 2 + core
        return pltpu.make_async_remote_copy(
            src_ref=slot(s, owner), dst_ref=slot(s, owner),
            send_sem=fwd_send.at[d - 1, s], recv_sem=fwd_recv.at[d - 1, s],
            device_id=dev(sibling, zi), device_id_type=MESH_ID)

    def forward(s):
        for d in range(1, chips):
            x_copy(d, s).wait_recv()
            fwd_copy(d, s).start()

    own_rows = 2 * blocks

    def one_sub(s, carry):
        def some_pulses(group, inner):
            turned = []
            for u in range(UNROLL):
                pulse = s * SUB + group * UNROLL + u
                amount = (LANES - (shifts[0, pulse] + (LANES - TAPS // 2 + 1))) & (LANES - 1)
                turned.append([
                    pltpu.roll(part, amount, axis=1)
                    for part in (
                        cells[pulse].astype(F32), left_f[pl.ds(2 * pulse, 2), :], right_f[pl.ds(2 * pulse, 2), :],
                    )
                ])
            for u in range(UNROLL):
                j = group * UNROLL + u
                rolled[pl.ds(j, own_rows, PITCH), :] = turned[u][0]
                rolled[pl.ds(own_rows * PITCH + j, 2, PITCH), :] = turned[u][1]
                rolled[pl.ds((own_rows + 2) * PITCH + j, 2, PITCH), :] = turned[u][2]
            return inner

        lax.fori_loop(0, SUB // UNROLL, some_pulses, 0)

        rows = pl.ds(pl.multiple_of(s * SUB, SUB), SUB)
        at = reach[rows, :]
        first = at < float(LANES)
        second = at < float(2 * LANES)
        turn_re, turn_im = d_re[rows, :], d_im[rows, :]
        now_re, now_im = e_re[rows, :], e_im[rows, :]

        def block(b, c):
            b = min(b, blocks + 1)
            where = own_rows if b == 0 else own_rows + 2 if b == blocks + 1 else 2 * (b - 1)
            return rolled[(where + c) * PITCH:(where + c) * PITCH + SUB, :]

        for b in range(blocks + 1):
            z = [
                jnp.where(first, block(b, c), jnp.where(second, block(b + 1, c), block(b + 2, c)))
                for c in range(2)
            ]
            span = slice(b * LANES, (b + 1) * LANES)
            y[0:SUB, span] = (now_re * z[0] - now_im * z[1]).astype(BF16)
            y[SUB:2 * SUB, span] = (now_im * z[0] + now_re * z[1]).astype(BF16)
            now_re, now_im = now_re * turn_re - now_im * turn_im, now_im * turn_re + now_re * turn_im

        taps_out[...] = jnp.dot(lhs[s], y[...], preferred_element_type=F32)
        width = (blocks + 1) * LANES
        total = taps_out[0:2 * BEAMS, :]
        for k in range(1, TAPS):
            total = total + pltpu.roll(taps_out[k * 2 * BEAMS:(k + 1) * 2 * BEAMS, :], width - k, axis=1)
        slot(s, me)[...] = total[:, :blocks * LANES].astype(BF16)

        for d in range(1, chips):
            x_copy(d, s).start()
        sib_copy(s).start()

        @pl.when(s >= LAG)
        def _():
            forward(s - LAG)

        return carry

    lax.fori_loop(0, subs, one_sub, 0)
    n_rows = n_pulse * subs * 2 * BEAMS
    row = lax.broadcasted_iota(jnp.int32, (n_rows, FOOT), 0)
    block_row = row // (2 * BEAMS)
    beam = ((block_row % n_pulse) * subs + block_row // n_pulse) * BEAMS + row % BEAMS
    is_im = (row // BEAMS) % 2
    for load in loads[7:]:
        load.wait()
    for t in range(TILE_DEV):
        ids = footprint[pl.ds(me * TILE_DEV + t, 1), :]
        hit = beam == ids
        hot_re = jnp.where(hit & (is_im == 0), 1.0, 0.0).astype(BF16)
        hot_im = jnp.where(hit & (is_im == 1), 1.0, 0.0).astype(BF16)
        c_re = jnp.transpose(coeffs[t, 0].astype(F32)).astype(BF16)
        c_im = jnp.transpose(coeffs[t, 1].astype(F32)).astype(BF16)

        def spread(a, b):
            return lax.dot_general(a, b, (((1,), (1,)), ((), ())), preferred_element_type=F32)

        dense[t * 2 * AZ:t * 2 * AZ + AZ, :] = (spread(c_re, hot_re) - spread(c_im, hot_im)).astype(BF16)
        dense[t * 2 * AZ + AZ:(t + 1) * 2 * AZ, :] = (spread(c_im, hot_re) + spread(c_re, hot_im)).astype(BF16)

    def landed(first, last):
        def one(s, carry):
            sib_copy(s).wait_recv()
            for d in range(1, chips):
                fwd_copy(d, s).wait_recv()
            return carry

        lax.fori_loop(first, last, one, 0)

    early = subs - LAG
    half = early * n_pulse * 2 * BEAMS
    pieces = blocks * LANES // COLUMNS

    def columns(n):
        return pl.ds(pl.multiple_of(n * COLUMNS, COLUMNS), COLUMNS)

    def first_half(n, carry):
        half_sum[:, columns(n)] = jnp.dot(
            dense[:, 0:half], gathered[0:half, columns(n)], preferred_element_type=F32)
        return carry

    def out_copy(n):
        return pltpu.make_async_copy(image.at[:, columns(n)], out.at[:, columns(n)], out_sem.at[n])

    def second_half(n, carry):
        image[:, columns(n)] = (half_sum[:, columns(n)] + jnp.dot(
            dense[:, half:n_rows], gathered[half:n_rows, columns(n)], preferred_element_type=F32)).astype(BF16)
        out_copy(n).start()
        return carry

    forward(early)
    landed(0, early)
    lax.fori_loop(0, pieces // 2, first_half, 0)
    forward(early + 1)
    lax.fori_loop(pieces // 2, pieces, first_half, 0)
    for s in range(early + 2, subs):
        forward(s)
    landed(early, subs)
    lax.fori_loop(0, pieces, second_half, 0)

    def finish(s, carry):
        sib_copy(s).wait_send()
        for d in range(1, chips):
            x_copy(d, s).wait_send()
            fwd_copy(d, s).wait_send()
        return carry

    lax.fori_loop(0, subs, finish, 0)

    def drain(n, carry):
        out_copy(n).wait()
        return carry

    lax.fori_loop(0, pieces, drain, 0)

    @pl.when(has_left)
    def _():
        to_left().wait_send()

    @pl.when(has_right)
    def _():
        to_right().wait_send()


def hand_out(image, out, sems):
    rows = image.shape[0] // COPIES
    copies = [
        pltpu.make_async_copy(image.at[n * rows:(n + 1) * rows], out.at[n * rows:(n + 1) * rows], sems.at[n])
        for n in range(COPIES)
    ]
    for copy in copies:
        copy.start()
    for copy in copies:
        copy.wait()


def body(n_pulse, n_range, echoes, shifts, tap_weights, angles, slopes, steering, footprint, tile_coeffs):
    pulses, _, width = echoes.shape
    blocks = width // LANES
    subs = pulses // SUB
    chips = n_pulse // 2
    by_block = echoes.reshape(pulses, 2, blocks, LANES).transpose(0, 2, 1, 3).reshape(pulses, 2 * blocks, LANES)
    heads = echoes[:, :, :LANES].reshape(2 * pulses, LANES)
    tails = echoes[:, :, width - LANES:].reshape(2 * pulses, LANES)
    n_rows = n_pulse * subs * 2 * BEAMS
    out_rows = TILE_DEV * 2 * AZ
    vmem = pl.BlockSpec(memory_space=pltpu.VMEM)
    hbm = pl.BlockSpec(memory_space=pltpu.HBM)
    dma = pltpu.SemaphoreType.DMA
    image = pl.pallas_call(
        functools.partial(beam_kernel, n_pulse, n_range, blocks, subs),
        out_shape=jax.ShapeDtypeStruct((out_rows, width), BF16),
        in_specs=[hbm] * 8 + [vmem] * 2,
        out_specs=hbm,
        scratch_shapes=[
            pltpu.VMEM((pulses, 2 * blocks, LANES), BF16),
            pltpu.SMEM((1, pulses), jnp.int32),
            pltpu.VMEM((1, pulses), jnp.int32),
            pltpu.VMEM((TAPS, pulses), F32),
            pltpu.VMEM((1, pulses), F32),
            pltpu.VMEM((1, pulses), F32),
            pltpu.VMEM((2 * BEAMS, SUB), BF16),
            pltpu.VMEM(footprint.shape, jnp.int32),
            pltpu.VMEM((TILE_DEV, 2, FOOT, AZ), BF16),
            pltpu.VMEM((2 * pulses, LANES), BF16),
            pltpu.VMEM((2 * pulses, LANES), BF16),
            pltpu.VMEM((2 * pulses, LANES), F32),
            pltpu.VMEM((2 * pulses, LANES), F32),
            pltpu.VMEM(((2 * blocks + 4) * PITCH, LANES), F32),
            pltpu.VMEM((2 * SUB, width + LANES), BF16),
            pltpu.VMEM((TAPS * 2 * BEAMS, width + LANES), F32),
            pltpu.VMEM((n_rows, width), BF16),
            pltpu.VMEM((out_rows, n_rows), BF16),
            pltpu.VMEM((out_rows, width), F32),
            pltpu.VMEM((out_rows, width), BF16),
            pltpu.VMEM((subs, TAPS * 2 * BEAMS, 2 * SUB), BF16),
            pltpu.VMEM((pulses, LANES), F32),
            pltpu.VMEM((pulses, LANES), F32),
            pltpu.VMEM((pulses, LANES), F32),
            pltpu.VMEM((pulses, LANES), F32),
            pltpu.VMEM((pulses, LANES), F32),
            dma((9,)),
            dma((2,)),
            dma((2,)),
            dma((width // COLUMNS,)),
            dma((chips - 1, subs)),
            dma((chips - 1, subs)),
            dma((subs,)),
            dma((subs,)),
            dma((chips - 1, subs)),
            dma((chips - 1, subs)),
        ],
        compiler_params=pltpu.CompilerParams(
            collective_id=0, has_side_effects=True, vmem_limit_bytes=63 * 1024 * 1024
        ),
    )(
        by_block, shifts[None], tap_weights.T, angles[None], slopes[None], steering.reshape(2 * BEAMS, SUB),
        footprint, tile_coeffs.transpose(0, 1, 3, 2), heads, tails,
    )
    image = pl.pallas_call(
        hand_out,
        out_shape=jax.ShapeDtypeStruct((out_rows, width), BF16),
        in_specs=[hbm],
        out_specs=hbm,
        scratch_shapes=[dma((COPIES,))],
        compiler_params=pltpu.CompilerParams(vmem_limit_bytes=63 * 1024 * 1024),
    )(image)
    return image.reshape(TILE_DEV, 2, AZ, width)


def solution(mesh):
    placed = (
        P(("groups", "pulse"), None, "range"),
        P(("groups", "pulse")),
        P(("groups", "pulse"), None),
        P(("groups", "pulse")),
        P(("groups", "pulse")),
        P(),
        P("groups", None),
        P(("groups", "pulse"), None, None, None),
    )
    return jax.shard_map(
        functools.partial(body, mesh.shape["pulse"], mesh.shape["range"]),
        mesh=mesh,
        in_specs=placed,
        out_specs=P(("groups", "pulse"), None, None, "range"),
        check_vma=False,
    )
```

```python
import functools

import jax
import jax.numpy as jnp
from jax import lax
from jax.experimental import pallas as pl
from jax.experimental.pallas import tpu as pltpu
from jax.sharding import PartitionSpec as P

SUB = 32
BEAMS = 8
TAPS = 8
TILE_DEV = 4
FOOT = 32
AZ = 64
LANES = 128
F32 = jnp.float32
BF16 = jnp.bfloat16
MESH_ID = pl.DeviceIdType.MESH
UNROLL = 8
LAG = 4
PITCH = SUB + 8
COPIES = 8
COLUMNS = 256


def beam_kernel(
    n_pulse, n_range, blocks, subs,
    echoes_in, shifts_in, taps_in, angles_in, slopes_in, steering_in, footprint_in, coeffs_in, heads, tails,
    out,
    cells, shifts, shift_row, taps, angles, slopes, steering, footprint, coeffs,
    left, right, left_f, right_f, rolled, y, taps_out, gathered, dense, half_sum, image,
    lhs, e_re, e_im, d_re, d_im, reach,
    load_sem, halo_send, halo_recv, out_sem,
    x_send, x_recv, sib_send, sib_recv, fwd_send, fwd_recv,
):
    chips = n_pulse // 2
    me = lax.axis_index("pulse")
    zi = lax.axis_index("range")
    gi = lax.axis_index("groups")
    chip = me // 2
    core = me % 2
    sibling = chip * 2 + (1 - core)
    pulses = subs * SUB
    has_left = zi > 0
    has_right = zi < n_range - 1

    def dev(p, z):
        return (gi, p, z)

    loads = [
        pltpu.make_async_copy(source, target, load_sem.at[n])
        for n, (source, target) in enumerate([
            (slopes_in, slopes), (taps_in, taps), (steering_in, steering), (angles_in, angles),
            (shifts_in, shift_row), (shifts_in, shifts), (echoes_in, cells),
            (footprint_in, footprint), (coeffs_in, coeffs),
        ])
    ]
    for load in loads:
        load.start()

    barrier = pltpu.get_barrier_semaphore()
    pl.semaphore_signal(barrier, inc=1, device_id=dev(sibling, zi), device_id_type=MESH_ID)
    for d in range(1, chips):
        peer = ((chip + d) % chips) * 2 + core
        pl.semaphore_signal(barrier, inc=1, device_id=dev(peer, zi), device_id_type=MESH_ID)

    @pl.when(has_left)
    def _():
        pl.semaphore_signal(barrier, inc=1, device_id=dev(me, zi - 1), device_id_type=MESH_ID)

    @pl.when(has_right)
    def _():
        pl.semaphore_signal(barrier, inc=1, device_id=dev(me, zi + 1), device_id_type=MESH_ID)

    pl.semaphore_wait(barrier, chips + jnp.minimum(zi, 1) + jnp.minimum(n_range - 1 - zi, 1))

    def to_left():
        return pltpu.make_async_remote_copy(
            src_ref=heads, dst_ref=right, send_sem=halo_send.at[0], recv_sem=halo_recv.at[0],
            device_id=dev(me, zi - 1), device_id_type=MESH_ID)

    def to_right():
        return pltpu.make_async_remote_copy(
            src_ref=tails, dst_ref=left, send_sem=halo_send.at[1], recv_sem=halo_recv.at[1],
            device_id=dev(me, zi + 1), device_id_type=MESH_ID)

    @pl.when(has_left)
    def _():
        to_left().start()

    @pl.when(has_right)
    def _():
        to_right().start()

    for load in loads[:3]:
        load.wait()
    tap_phase = slopes[...] * lax.broadcasted_iota(jnp.int32, (TAPS, pulses), 0).astype(F32)
    tap_re = taps[...] * jnp.cos(tap_phase)
    tap_im = -taps[...] * jnp.sin(tap_phase)
    weights = steering[...].astype(F32)
    st_re = jnp.concatenate([weights[0:BEAMS]] * subs, axis=1)
    st_im = jnp.concatenate([weights[BEAMS:2 * BEAMS]] * subs, axis=1)
    from_re, from_im = [], []
    for k in range(TAPS):
        w_re = st_re * tap_re[k:k + 1] - st_im * tap_im[k:k + 1]
        w_im = st_re * tap_im[k:k + 1] + st_im * tap_re[k:k + 1]
        from_re += [w_re, w_im]
        from_im += [-w_im, w_re]
    from_re = jnp.concatenate(from_re, axis=0)
    from_im = jnp.concatenate(from_im, axis=0)
    on_re = lax.broadcasted_iota(jnp.int32, (TAPS * 2 * BEAMS, LANES), 1) < SUB
    for s in range(subs):
        first = s * SUB // LANES * LANES
        off = s * SUB - first
        part_re = pltpu.roll(from_re[:, first:first + LANES], (LANES - off) % LANES, axis=1)
        part_im = pltpu.roll(from_im[:, first:first + LANES], (LANES + SUB - off) % LANES, axis=1)
        lhs[s] = jnp.where(on_re, part_re, part_im)[:, :2 * SUB].astype(BF16)

    for load in loads[3:5]:
        load.wait()
    lane = lax.broadcasted_iota(jnp.int32, (LANES, LANES), 1).astype(F32)
    start = (zi * (blocks * LANES)).astype(F32)
    shift_values = shift_row[...].astype(F32)
    step = slopes[...] * float(LANES)
    step_re, step_im = jnp.cos(step), jnp.sin(step)
    for h in range(pulses // LANES):
        span = slice(h * LANES, (h + 1) * LANES)

        def column(row):
            return jnp.transpose(jnp.broadcast_to(row[:, span], (LANES, LANES)))

        phase = column(angles[...]) + column(slopes[...]) * (start + lane)
        e_re[span, :] = jnp.cos(phase)
        e_im[span, :] = jnp.sin(phase)
        d_re[span, :] = column(step_re)
        d_im[span, :] = column(step_im)
        reach[span, :] = column(shift_values) + lane + float(LANES - TAPS // 2 + 1)

    @pl.when(has_left)
    def _():
        to_right().wait_recv()

    @pl.when(has_right)
    def _():
        to_left().wait_recv()

    @pl.when(jnp.logical_not(has_left))
    def _():
        left[...] = jnp.zeros(left.shape, BF16)

    @pl.when(jnp.logical_not(has_right))
    def _():
        right[...] = jnp.zeros(right.shape, BF16)

    left_f[...] = left[...].astype(F32)
    right_f[...] = right[...].astype(F32)
    for load in loads[5:7]:
        load.wait()

    def slot(s, owner):
        return gathered.at[pl.ds(pl.multiple_of((s * n_pulse + owner) * 2 * BEAMS, 2 * BEAMS), 2 * BEAMS), :]

    def x_copy(d, s):
        peer = ((chip + d) % chips) * 2 + core
        return pltpu.make_async_remote_copy(
            src_ref=slot(s, me), dst_ref=slot(s, me),
            send_sem=x_send.at[d - 1, s], recv_sem=x_recv.at[d - 1, s],
            device_id=dev(peer, zi), device_id_type=MESH_ID)

    def sib_copy(s):
        return pltpu.make_async_remote_copy(
            src_ref=slot(s, me), dst_ref=slot(s, me),
            send_sem=sib_send.at[s], recv_sem=sib_recv.at[s],
            device_id=dev(sibling, zi), device_id_type=MESH_ID)

    def fwd_copy(d, s):
        owner = ((chip + chips - d) % chips) * 2 + core
        return pltpu.make_async_remote_copy(
            src_ref=slot(s, owner), dst_ref=slot(s, owner),
            send_sem=fwd_send.at[d - 1, s], recv_sem=fwd_recv.at[d - 1, s],
            device_id=dev(sibling, zi), device_id_type=MESH_ID)

    def forward(s):
        for d in range(1, chips):
            x_copy(d, s).wait_recv()
            fwd_copy(d, s).start()

    own_rows = 2 * blocks

    def one_sub(s, carry):
        def some_pulses(group, inner):
            turned = []
            for u in range(UNROLL):
                pulse = s * SUB + group * UNROLL + u
                amount = (LANES - (shifts[0, pulse] + (LANES - TAPS // 2 + 1))) & (LANES - 1)
                turned.append([
                    pltpu.roll(part, amount, axis=1)
                    for part in (
                        cells[pulse].astype(F32), left_f[pl.ds(2 * pulse, 2), :], right_f[pl.ds(2 * pulse, 2), :],
                    )
                ])
            for u in range(UNROLL):
                j = group * UNROLL + u
                rolled[pl.ds(j, own_rows, PITCH), :] = turned[u][0]
                rolled[pl.ds(own_rows * PITCH + j, 2, PITCH), :] = turned[u][1]
                rolled[pl.ds((own_rows + 2) * PITCH + j, 2, PITCH), :] = turned[u][2]
            return inner

        lax.fori_loop(0, SUB // UNROLL, some_pulses, 0)

        rows = pl.ds(pl.multiple_of(s * SUB, SUB), SUB)
        at = reach[rows, :]
        first = at < float(LANES)
        second = at < float(2 * LANES)
        turn_re, turn_im = d_re[rows, :], d_im[rows, :]
        now_re, now_im = e_re[rows, :], e_im[rows, :]

        def block(b, c):
            b = min(b, blocks + 1)
            where = own_rows if b == 0 else own_rows + 2 if b == blocks + 1 else 2 * (b - 1)
            return rolled[(where + c) * PITCH:(where + c) * PITCH + SUB, :]

        for b in range(blocks + 1):
            z = [
                jnp.where(first, block(b, c), jnp.where(second, block(b + 1, c), block(b + 2, c)))
                for c in range(2)
            ]
            span = slice(b * LANES, (b + 1) * LANES)
            y[0:SUB, span] = (now_re * z[0] - now_im * z[1]).astype(BF16)
            y[SUB:2 * SUB, span] = (now_im * z[0] + now_re * z[1]).astype(BF16)
            now_re, now_im = now_re * turn_re - now_im * turn_im, now_im * turn_re + now_re * turn_im

        taps_out[...] = jnp.dot(lhs[s], y[...], preferred_element_type=F32)
        width = (blocks + 1) * LANES
        total = taps_out[0:2 * BEAMS, :]
        for k in range(1, TAPS):
            total = total + pltpu.roll(taps_out[k * 2 * BEAMS:(k + 1) * 2 * BEAMS, :], width - k, axis=1)
        slot(s, me)[...] = total[:, :blocks * LANES].astype(BF16)

        for d in range(1, chips):
            x_copy(d, s).start()
        sib_copy(s).start()

        @pl.when(s >= LAG)
        def _():
            forward(s - LAG)

        return carry

    lax.fori_loop(0, subs, one_sub, 0)
    n_rows = n_pulse * subs * 2 * BEAMS
    row = lax.broadcasted_iota(jnp.int32, (n_rows, FOOT), 0)
    block_row = row // (2 * BEAMS)
    beam = ((block_row % n_pulse) * subs + block_row // n_pulse) * BEAMS + row % BEAMS
    is_im = (row // BEAMS) % 2
    for load in loads[7:]:
        load.wait()
    for t in range(TILE_DEV):
        ids = footprint[pl.ds(me * TILE_DEV + t, 1), :]
        hit = beam == ids
        hot_re = jnp.where(hit & (is_im == 0), 1.0, 0.0).astype(BF16)
        hot_im = jnp.where(hit & (is_im == 1), 1.0, 0.0).astype(BF16)
        c_re = jnp.transpose(coeffs[t, 0].astype(F32)).astype(BF16)
        c_im = jnp.transpose(coeffs[t, 1].astype(F32)).astype(BF16)

        def spread(a, b):
            return lax.dot_general(a, b, (((1,), (1,)), ((), ())), preferred_element_type=F32)

        dense[t * 2 * AZ:t * 2 * AZ + AZ, :] = (spread(c_re, hot_re) - spread(c_im, hot_im)).astype(BF16)
        dense[t * 2 * AZ + AZ:(t + 1) * 2 * AZ, :] = (spread(c_im, hot_re) + spread(c_re, hot_im)).astype(BF16)

    def landed(first, last):
        def one(s, carry):
            sib_copy(s).wait_recv()
            for d in range(1, chips):
                fwd_copy(d, s).wait_recv()
            return carry

        lax.fori_loop(first, last, one, 0)

    early = subs - LAG
    half = early * n_pulse * 2 * BEAMS
    pieces = blocks * LANES // COLUMNS

    def columns(n):
        return pl.ds(pl.multiple_of(n * COLUMNS, COLUMNS), COLUMNS)

    def first_half(n, carry):
        half_sum[:, columns(n)] = jnp.dot(
            dense[:, 0:half], gathered[0:half, columns(n)], preferred_element_type=F32)
        return carry

    def out_copy(n):
        return pltpu.make_async_copy(image.at[:, columns(n)], out.at[:, columns(n)], out_sem.at[n])

    def second_half(n, carry):
        image[:, columns(n)] = (half_sum[:, columns(n)] + jnp.dot(
            dense[:, half:n_rows], gathered[half:n_rows, columns(n)], preferred_element_type=F32)).astype(BF16)
        out_copy(n).start()
        return carry

    forward(early)
    landed(0, early)
    lax.fori_loop(0, pieces // 2, first_half, 0)
    forward(early + 1)
    lax.fori_loop(pieces // 2, pieces, first_half, 0)
    for s in range(early + 2, subs):
        forward(s)
    landed(early, subs)
    lax.fori_loop(0, pieces, second_half, 0)

    def finish(s, carry):
        sib_copy(s).wait_send()
        for d in range(1, chips):
            x_copy(d, s).wait_send()
            fwd_copy(d, s).wait_send()
        return carry

    lax.fori_loop(0, subs, finish, 0)

    def drain(n, carry):
        out_copy(n).wait()
        return carry

    lax.fori_loop(0, pieces, drain, 0)

    @pl.when(has_left)
    def _():
        to_left().wait_send()

    @pl.when(has_right)
    def _():
        to_right().wait_send()


def hand_out(image, out, held, in_sems, out_sems):
    rows = image.shape[0] // COPIES
    into, onward = [], []
    for n in range(COPIES):
        part = slice(n * rows, (n + 1) * rows)
        into.append(pltpu.make_async_copy(image.at[part], held.at[part], in_sems.at[n]))
        onward.append(pltpu.make_async_copy(held.at[part], out.at[part], out_sems.at[n]))
    for copy in into:
        copy.start()
    for first, second in zip(into, onward):
        first.wait()
        second.start()
    for copy in onward:
        copy.wait()


def body(n_pulse, n_range, echoes, shifts, tap_weights, angles, slopes, steering, footprint, tile_coeffs):
    pulses, _, width = echoes.shape
    blocks = width // LANES
    subs = pulses // SUB
    chips = n_pulse // 2
    by_block = echoes.reshape(pulses, 2, blocks, LANES).transpose(0, 2, 1, 3).reshape(pulses, 2 * blocks, LANES)
    heads = echoes[:, :, :LANES].reshape(2 * pulses, LANES)
    tails = echoes[:, :, width - LANES:].reshape(2 * pulses, LANES)
    n_rows = n_pulse * subs * 2 * BEAMS
    out_rows = TILE_DEV * 2 * AZ
    vmem = pl.BlockSpec(memory_space=pltpu.VMEM)
    hbm = pl.BlockSpec(memory_space=pltpu.HBM)
    dma = pltpu.SemaphoreType.DMA
    image = pl.pallas_call(
        functools.partial(beam_kernel, n_pulse, n_range, blocks, subs),
        out_shape=jax.ShapeDtypeStruct((out_rows, width), BF16),
        in_specs=[hbm] * 8 + [vmem] * 2,
        out_specs=hbm,
        scratch_shapes=[
            pltpu.VMEM((pulses, 2 * blocks, LANES), BF16),
            pltpu.SMEM((1, pulses), jnp.int32),
            pltpu.VMEM((1, pulses), jnp.int32),
            pltpu.VMEM((TAPS, pulses), F32),
            pltpu.VMEM((1, pulses), F32),
            pltpu.VMEM((1, pulses), F32),
            pltpu.VMEM((2 * BEAMS, SUB), BF16),
            pltpu.VMEM(footprint.shape, jnp.int32),
            pltpu.VMEM((TILE_DEV, 2, FOOT, AZ), BF16),
            pltpu.VMEM((2 * pulses, LANES), BF16),
            pltpu.VMEM((2 * pulses, LANES), BF16),
            pltpu.VMEM((2 * pulses, LANES), F32),
            pltpu.VMEM((2 * pulses, LANES), F32),
            pltpu.VMEM(((2 * blocks + 4) * PITCH, LANES), F32),
            pltpu.VMEM((2 * SUB, width + LANES), BF16),
            pltpu.VMEM((TAPS * 2 * BEAMS, width + LANES), F32),
            pltpu.VMEM((n_rows, width), BF16),
            pltpu.VMEM((out_rows, n_rows), BF16),
            pltpu.VMEM((out_rows, width), F32),
            pltpu.VMEM((out_rows, width), BF16),
            pltpu.VMEM((subs, TAPS * 2 * BEAMS, 2 * SUB), BF16),
            pltpu.VMEM((pulses, LANES), F32),
            pltpu.VMEM((pulses, LANES), F32),
            pltpu.VMEM((pulses, LANES), F32),
            pltpu.VMEM((pulses, LANES), F32),
            pltpu.VMEM((pulses, LANES), F32),
            dma((9,)),
            dma((2,)),
            dma((2,)),
            dma((width // COLUMNS,)),
            dma((chips - 1, subs)),
            dma((chips - 1, subs)),
            dma((subs,)),
            dma((subs,)),
            dma((chips - 1, subs)),
            dma((chips - 1, subs)),
        ],
        compiler_params=pltpu.CompilerParams(
            collective_id=0, has_side_effects=True, vmem_limit_bytes=63 * 1024 * 1024
        ),
    )(
        by_block, shifts[None], tap_weights.T, angles[None], slopes[None], steering.reshape(2 * BEAMS, SUB),
        footprint, tile_coeffs.transpose(0, 1, 3, 2), heads, tails,
    )
    image = pl.pallas_call(
        hand_out,
        out_shape=jax.ShapeDtypeStruct((out_rows, width), BF16),
        in_specs=[hbm],
        out_specs=hbm,
        scratch_shapes=[pltpu.VMEM((out_rows, width), BF16), dma((COPIES,)), dma((COPIES,))],
        compiler_params=pltpu.CompilerParams(vmem_limit_bytes=63 * 1024 * 1024),
    )(image)
    return image.reshape(TILE_DEV, 2, AZ, width)


def solution(mesh):
    placed = (
        P(("groups", "pulse"), None, "range"),
        P(("groups", "pulse")),
        P(("groups", "pulse"), None),
        P(("groups", "pulse")),
        P(("groups", "pulse")),
        P(),
        P("groups", None),
        P(("groups", "pulse"), None, None, None),
    )
    return jax.shard_map(
        functools.partial(body, mesh.shape["pulse"], mesh.shape["range"]),
        mesh=mesh,
        in_specs=placed,
        out_specs=P(("groups", "pulse"), None, None, "range"),
        check_vma=False,
    )
```

```python
import functools

import jax
import jax.numpy as jnp
from jax import lax
from jax.experimental import pallas as pl
from jax.experimental.pallas import tpu as pltpu
from jax.sharding import PartitionSpec as P

SUB = 32
BEAMS = 8
TAPS = 8
TILE_DEV = 4
FOOT = 32
AZ = 64
LANES = 128
F32 = jnp.float32
BF16 = jnp.bfloat16
MESH_ID = pl.DeviceIdType.MESH
UNROLL = 8
LAG = 4
PITCH = SUB + 8
COPIES = 8
COLUMNS = 256


def beam_kernel(
    n_pulse, n_range, blocks, subs,
    echoes_in, shifts_in, taps_in, angles_in, slopes_in, steering_in, footprint_in, coeffs_in, heads, tails,
    out,
    cells, shifts, shift_row, taps, angles, slopes, steering, footprint, coeffs,
    left, right, left_f, right_f, rolled, y, taps_out, gathered, dense, half_sum, image,
    lhs, e_re, e_im, d_re, d_im, reach,
    load_sem, halo_send, halo_recv, out_sem,
    x_send, x_recv, sib_send, sib_recv, fwd_send, fwd_recv,
):
    chips = n_pulse // 2
    me = lax.axis_index("pulse")
    zi = lax.axis_index("range")
    gi = lax.axis_index("groups")
    chip = me // 2
    core = me % 2
    sibling = chip * 2 + (1 - core)
    pulses = subs * SUB
    has_left = zi > 0
    has_right = zi < n_range - 1

    def dev(p, z):
        return (gi, p, z)

    loads = [
        pltpu.make_async_copy(source, target, load_sem.at[n])
        for n, (source, target) in enumerate([
            (slopes_in, slopes), (taps_in, taps), (steering_in, steering), (angles_in, angles),
            (shifts_in, shift_row), (shifts_in, shifts), (echoes_in, cells),
            (footprint_in, footprint), (coeffs_in, coeffs),
        ])
    ]
    for load in loads:
        load.start()

    barrier = pltpu.get_barrier_semaphore()
    pl.semaphore_signal(barrier, inc=1, device_id=dev(sibling, zi), device_id_type=MESH_ID)
    for d in range(1, chips):
        peer = ((chip + d) % chips) * 2 + core
        pl.semaphore_signal(barrier, inc=1, device_id=dev(peer, zi), device_id_type=MESH_ID)

    @pl.when(has_left)
    def _():
        pl.semaphore_signal(barrier, inc=1, device_id=dev(me, zi - 1), device_id_type=MESH_ID)

    @pl.when(has_right)
    def _():
        pl.semaphore_signal(barrier, inc=1, device_id=dev(me, zi + 1), device_id_type=MESH_ID)

    pl.semaphore_wait(barrier, chips + jnp.minimum(zi, 1) + jnp.minimum(n_range - 1 - zi, 1))

    def to_left():
        return pltpu.make_async_remote_copy(
            src_ref=heads, dst_ref=right, send_sem=halo_send.at[0], recv_sem=halo_recv.at[0],
            device_id=dev(me, zi - 1), device_id_type=MESH_ID)

    def to_right():
        return pltpu.make_async_remote_copy(
            src_ref=tails, dst_ref=left, send_sem=halo_send.at[1], recv_sem=halo_recv.at[1],
            device_id=dev(me, zi + 1), device_id_type=MESH_ID)

    @pl.when(has_left)
    def _():
        to_left().start()

    @pl.when(has_right)
    def _():
        to_right().start()

    for load in loads[:3]:
        load.wait()
    tap_phase = slopes[...] * lax.broadcasted_iota(jnp.int32, (TAPS, pulses), 0).astype(F32)
    tap_re = taps[...] * jnp.cos(tap_phase)
    tap_im = -taps[...] * jnp.sin(tap_phase)
    weights = steering[...].astype(F32)
    st_re = jnp.concatenate([weights[0:BEAMS]] * subs, axis=1)
    st_im = jnp.concatenate([weights[BEAMS:2 * BEAMS]] * subs, axis=1)
    from_re, from_im = [], []
    for k in range(TAPS):
        w_re = st_re * tap_re[k:k + 1] - st_im * tap_im[k:k + 1]
        w_im = st_re * tap_im[k:k + 1] + st_im * tap_re[k:k + 1]
        from_re += [w_re, w_im]
        from_im += [-w_im, w_re]
    from_re = jnp.concatenate(from_re, axis=0)
    from_im = jnp.concatenate(from_im, axis=0)
    on_re = lax.broadcasted_iota(jnp.int32, (TAPS * 2 * BEAMS, LANES), 1) < SUB
    for s in range(subs):
        first = s * SUB // LANES * LANES
        off = s * SUB - first
        part_re = pltpu.roll(from_re[:, first:first + LANES], (LANES - off) % LANES, axis=1)
        part_im = pltpu.roll(from_im[:, first:first + LANES], (LANES + SUB - off) % LANES, axis=1)
        lhs[s] = jnp.where(on_re, part_re, part_im)[:, :2 * SUB].astype(BF16)

    for load in loads[3:5]:
        load.wait()
    lane = lax.broadcasted_iota(jnp.int32, (LANES, LANES), 1).astype(F32)
    start = (zi * (blocks * LANES)).astype(F32)
    shift_values = shift_row[...].astype(F32)
    step = slopes[...] * float(LANES)
    step_re, step_im = jnp.cos(step), jnp.sin(step)
    for h in range(pulses // LANES):
        span = slice(h * LANES, (h + 1) * LANES)

        def column(row):
            return jnp.transpose(jnp.broadcast_to(row[:, span], (LANES, LANES)))

        phase = column(angles[...]) + column(slopes[...]) * (start + lane)
        e_re[span, :] = jnp.cos(phase)
        e_im[span, :] = jnp.sin(phase)
        d_re[span, :] = column(step_re)
        d_im[span, :] = column(step_im)
        reach[span, :] = column(shift_values) + lane + float(LANES - TAPS // 2 + 1)

    n_rows = n_pulse * subs * 2 * BEAMS
    row = lax.broadcasted_iota(jnp.int32, (n_rows, FOOT), 0)
    block_row = row // (2 * BEAMS)
    beam = ((block_row % n_pulse) * subs + block_row // n_pulse) * BEAMS + row % BEAMS
    is_im = (row // BEAMS) % 2
    for load in loads[7:]:
        load.wait()
    for t in range(TILE_DEV):
        ids = footprint[pl.ds(me * TILE_DEV + t, 1), :]
        hit = beam == ids
        hot_re = jnp.where(hit & (is_im == 0), 1.0, 0.0).astype(BF16)
        hot_im = jnp.where(hit & (is_im == 1), 1.0, 0.0).astype(BF16)
        c_re = jnp.transpose(coeffs[t, 0].astype(F32)).astype(BF16)
        c_im = jnp.transpose(coeffs[t, 1].astype(F32)).astype(BF16)

        def spread(a, b):
            return lax.dot_general(a, b, (((1,), (1,)), ((), ())), preferred_element_type=F32)

        dense[t * 2 * AZ:t * 2 * AZ + AZ, :] = (spread(c_re, hot_re) - spread(c_im, hot_im)).astype(BF16)
        dense[t * 2 * AZ + AZ:(t + 1) * 2 * AZ, :] = (spread(c_im, hot_re) + spread(c_re, hot_im)).astype(BF16)

    @pl.when(has_left)
    def _():
        to_right().wait_recv()

    @pl.when(has_right)
    def _():
        to_left().wait_recv()

    @pl.when(jnp.logical_not(has_left))
    def _():
        left[...] = jnp.zeros(left.shape, BF16)

    @pl.when(jnp.logical_not(has_right))
    def _():
        right[...] = jnp.zeros(right.shape, BF16)

    left_f[...] = left[...].astype(F32)
    right_f[...] = right[...].astype(F32)
    for load in loads[5:7]:
        load.wait()

    def slot(s, owner):
        return gathered.at[pl.ds(pl.multiple_of((s * n_pulse + owner) * 2 * BEAMS, 2 * BEAMS), 2 * BEAMS), :]

    def x_copy(d, s):
        peer = ((chip + d) % chips) * 2 + core
        return pltpu.make_async_remote_copy(
            src_ref=slot(s, me), dst_ref=slot(s, me),
            send_sem=x_send.at[d - 1, s], recv_sem=x_recv.at[d - 1, s],
            device_id=dev(peer, zi), device_id_type=MESH_ID)

    def sib_copy(s):
        return pltpu.make_async_remote_copy(
            src_ref=slot(s, me), dst_ref=slot(s, me),
            send_sem=sib_send.at[s], recv_sem=sib_recv.at[s],
            device_id=dev(sibling, zi), device_id_type=MESH_ID)

    def fwd_copy(d, s):
        owner = ((chip + chips - d) % chips) * 2 + core
        return pltpu.make_async_remote_copy(
            src_ref=slot(s, owner), dst_ref=slot(s, owner),
            send_sem=fwd_send.at[d - 1, s], recv_sem=fwd_recv.at[d - 1, s],
            device_id=dev(sibling, zi), device_id_type=MESH_ID)

    def forward(s):
        for d in range(1, chips):
            x_copy(d, s).wait_recv()
            fwd_copy(d, s).start()

    own_rows = 2 * blocks

    def one_sub(s, carry):
        def some_pulses(group, inner):
            turned = []
            for u in range(UNROLL):
                pulse = s * SUB + group * UNROLL + u
                amount = (LANES - (shifts[0, pulse] + (LANES - TAPS // 2 + 1))) & (LANES - 1)
                turned.append([
                    pltpu.roll(part, amount, axis=1)
                    for part in (
                        cells[pulse].astype(F32), left_f[pl.ds(2 * pulse, 2), :], right_f[pl.ds(2 * pulse, 2), :],
                    )
                ])
            for u in range(UNROLL):
                j = group * UNROLL + u
                rolled[pl.ds(j, own_rows, PITCH), :] = turned[u][0]
                rolled[pl.ds(own_rows * PITCH + j, 2, PITCH), :] = turned[u][1]
                rolled[pl.ds((own_rows + 2) * PITCH + j, 2, PITCH), :] = turned[u][2]
            return inner

        lax.fori_loop(0, SUB // UNROLL, some_pulses, 0)

        rows = pl.ds(pl.multiple_of(s * SUB, SUB), SUB)
        at = reach[rows, :]
        first = at < float(LANES)
        second = at < float(2 * LANES)
        turn_re, turn_im = d_re[rows, :], d_im[rows, :]
        now_re, now_im = e_re[rows, :], e_im[rows, :]

        def block(b, c):
            b = min(b, blocks + 1)
            where = own_rows if b == 0 else own_rows + 2 if b == blocks + 1 else 2 * (b - 1)
            return rolled[(where + c) * PITCH:(where + c) * PITCH + SUB, :]

        for b in range(blocks + 1):
            z = [
                jnp.where(first, block(b, c), jnp.where(second, block(b + 1, c), block(b + 2, c)))
                for c in range(2)
            ]
            span = slice(b * LANES, (b + 1) * LANES)
            y[0:SUB, span] = (now_re * z[0] - now_im * z[1]).astype(BF16)
            y[SUB:2 * SUB, span] = (now_im * z[0] + now_re * z[1]).astype(BF16)
            now_re, now_im = now_re * turn_re - now_im * turn_im, now_im * turn_re + now_re * turn_im

        taps_out[...] = jnp.dot(lhs[s], y[...], preferred_element_type=F32)
        width = (blocks + 1) * LANES
        total = taps_out[0:2 * BEAMS, :]
        for k in range(1, TAPS):
            total = total + pltpu.roll(taps_out[k * 2 * BEAMS:(k + 1) * 2 * BEAMS, :], width - k, axis=1)
        slot(s, me)[...] = total[:, :blocks * LANES].astype(BF16)

        for d in range(1, chips):
            x_copy(d, s).start()
        sib_copy(s).start()

        @pl.when(s >= LAG)
        def _():
            forward(s - LAG)

        return carry

    lax.fori_loop(0, subs, one_sub, 0)
    def landed(first, last):
        def one(s, carry):
            sib_copy(s).wait_recv()
            for d in range(1, chips):
                fwd_copy(d, s).wait_recv()
            return carry

        lax.fori_loop(first, last, one, 0)

    early = subs - LAG
    half = early * n_pulse * 2 * BEAMS
    pieces = blocks * LANES // COLUMNS

    def columns(n):
        return pl.ds(pl.multiple_of(n * COLUMNS, COLUMNS), COLUMNS)

    def first_half(n, carry):
        half_sum[:, columns(n)] = jnp.dot(
            dense[:, 0:half], gathered[0:half, columns(n)], preferred_element_type=F32)
        return carry

    def out_copy(n):
        return pltpu.make_async_copy(image.at[:, columns(n)], out.at[:, columns(n)], out_sem.at[n])

    def second_half(n, carry):
        image[:, columns(n)] = (half_sum[:, columns(n)] + jnp.dot(
            dense[:, half:n_rows], gathered[half:n_rows, columns(n)], preferred_element_type=F32)).astype(BF16)
        out_copy(n).start()
        return carry

    forward(early)
    landed(0, early)
    lax.fori_loop(0, pieces // 2, first_half, 0)
    forward(early + 1)
    lax.fori_loop(pieces // 2, pieces, first_half, 0)
    for s in range(early + 2, subs):
        forward(s)
    landed(early, subs)
    lax.fori_loop(0, pieces, second_half, 0)

    def finish(s, carry):
        sib_copy(s).wait_send()
        for d in range(1, chips):
            x_copy(d, s).wait_send()
            fwd_copy(d, s).wait_send()
        return carry

    lax.fori_loop(0, subs, finish, 0)

    def drain(n, carry):
        out_copy(n).wait()
        return carry

    lax.fori_loop(0, pieces, drain, 0)

    @pl.when(has_left)
    def _():
        to_left().wait_send()

    @pl.when(has_right)
    def _():
        to_right().wait_send()


def hand_out(image, out, held, in_sems, out_sems):
    rows = image.shape[0] // COPIES
    into, onward = [], []
    for n in range(COPIES):
        part = slice(n * rows, (n + 1) * rows)
        into.append(pltpu.make_async_copy(image.at[part], held.at[part], in_sems.at[n]))
        onward.append(pltpu.make_async_copy(held.at[part], out.at[part], out_sems.at[n]))
    for copy in into:
        copy.start()
    for first, second in zip(into, onward):
        first.wait()
        second.start()
    for copy in onward:
        copy.wait()


def body(n_pulse, n_range, echoes, shifts, tap_weights, angles, slopes, steering, footprint, tile_coeffs):
    pulses, _, width = echoes.shape
    blocks = width // LANES
    subs = pulses // SUB
    chips = n_pulse // 2
    by_block = echoes.reshape(pulses, 2, blocks, LANES).transpose(0, 2, 1, 3).reshape(pulses, 2 * blocks, LANES)
    heads = echoes[:, :, :LANES].reshape(2 * pulses, LANES)
    tails = echoes[:, :, width - LANES:].reshape(2 * pulses, LANES)
    n_rows = n_pulse * subs * 2 * BEAMS
    out_rows = TILE_DEV * 2 * AZ
    vmem = pl.BlockSpec(memory_space=pltpu.VMEM)
    hbm = pl.BlockSpec(memory_space=pltpu.HBM)
    dma = pltpu.SemaphoreType.DMA
    image = pl.pallas_call(
        functools.partial(beam_kernel, n_pulse, n_range, blocks, subs),
        out_shape=jax.ShapeDtypeStruct((out_rows, width), BF16),
        in_specs=[hbm] * 8 + [vmem] * 2,
        out_specs=hbm,
        scratch_shapes=[
            pltpu.VMEM((pulses, 2 * blocks, LANES), BF16),
            pltpu.SMEM((1, pulses), jnp.int32),
            pltpu.VMEM((1, pulses), jnp.int32),
            pltpu.VMEM((TAPS, pulses), F32),
            pltpu.VMEM((1, pulses), F32),
            pltpu.VMEM((1, pulses), F32),
            pltpu.VMEM((2 * BEAMS, SUB), BF16),
            pltpu.VMEM(footprint.shape, jnp.int32),
            pltpu.VMEM((TILE_DEV, 2, FOOT, AZ), BF16),
            pltpu.VMEM((2 * pulses, LANES), BF16),
            pltpu.VMEM((2 * pulses, LANES), BF16),
            pltpu.VMEM((2 * pulses, LANES), F32),
            pltpu.VMEM((2 * pulses, LANES), F32),
            pltpu.VMEM(((2 * blocks + 4) * PITCH, LANES), F32),
            pltpu.VMEM((2 * SUB, width + LANES), BF16),
            pltpu.VMEM((TAPS * 2 * BEAMS, width + LANES), F32),
            pltpu.VMEM((n_rows, width), BF16),
            pltpu.VMEM((out_rows, n_rows), BF16),
            pltpu.VMEM((out_rows, width), F32),
            pltpu.VMEM((out_rows, width), BF16),
            pltpu.VMEM((subs, TAPS * 2 * BEAMS, 2 * SUB), BF16),
            pltpu.VMEM((pulses, LANES), F32),
            pltpu.VMEM((pulses, LANES), F32),
            pltpu.VMEM((pulses, LANES), F32),
            pltpu.VMEM((pulses, LANES), F32),
            pltpu.VMEM((pulses, LANES), F32),
            dma((9,)),
            dma((2,)),
            dma((2,)),
            dma((width // COLUMNS,)),
            dma((chips - 1, subs)),
            dma((chips - 1, subs)),
            dma((subs,)),
            dma((subs,)),
            dma((chips - 1, subs)),
            dma((chips - 1, subs)),
        ],
        compiler_params=pltpu.CompilerParams(
            collective_id=0, has_side_effects=True, vmem_limit_bytes=63 * 1024 * 1024
        ),
    )(
        by_block, shifts[None], tap_weights.T, angles[None], slopes[None], steering.reshape(2 * BEAMS, SUB),
        footprint, tile_coeffs.transpose(0, 1, 3, 2), heads, tails,
    )
    image = pl.pallas_call(
        hand_out,
        out_shape=jax.ShapeDtypeStruct((out_rows, width), BF16),
        in_specs=[hbm],
        out_specs=hbm,
        scratch_shapes=[pltpu.VMEM((out_rows, width), BF16), dma((COPIES,)), dma((COPIES,))],
        compiler_params=pltpu.CompilerParams(vmem_limit_bytes=63 * 1024 * 1024),
    )(image)
    return image.reshape(TILE_DEV, 2, AZ, width)


def solution(mesh):
    placed = (
        P(("groups", "pulse"), None, "range"),
        P(("groups", "pulse")),
        P(("groups", "pulse"), None),
        P(("groups", "pulse")),
        P(("groups", "pulse")),
        P(),
        P("groups", None),
        P(("groups", "pulse"), None, None, None),
    )
    return jax.shard_map(
        functools.partial(body, mesh.shape["pulse"], mesh.shape["range"]),
        mesh=mesh,
        in_specs=placed,
        out_specs=P(("groups", "pulse"), None, None, "range"),
        check_vma=False,
    )
```
